512 devices in a mesh: lon: 32 (over z, x_hi), chan: 16 (over x_lo, y, core).
Axes of the slice: x: 4 (x_hi: 2, x_lo: 2; x = x_hi * 2 + x_lo), y: 4, z: 16, core: 2. Of those that a mesh axis runs over, the one named last changes fastest.
Arguments:
- features: bfloat16 [48, 256, 2048], P(None, 'lon', 'chan'), may hold values from -6 to 6
- w_point: bfloat16 [2048, 256], P('chan'), may hold values from -0.125 to 0.125
- w_dilated: bfloat16 [3, 3, 3, 2048, 256], P(None, None, None, 'chan'), may hold values from -0.046875 to 0.046875
- w_pool: bfloat16 [2048, 256], P('chan'), may hold values from -0.125 to 0.125
- bn_scale: float32 [5, 256], replicated, may hold values from 0.25 to 1.75
- bn_shift: float32 [5, 256], replicated, may hold values from -3 to 3
- proj_weight: bfloat16 [5, 256, 256], P(None, None, 'chan'), may hold values from -0.15625 to 0.15625
- proj_scale: float32 [256], P('chan'), may hold values from 0.25 to 1.75
- proj_shift: float32 [256], P('chan'), may hold values from -3 to 3
- skip: bfloat16 [48, 256, 48], P(None, 'lon'), may hold values from -6 to 6
- merge_weight: bfloat16 [3, 3, 304, 256], P(None, None, None, 'chan'), may hold values from -0.109375 to 0.109375
- merge_scale: float32 [256], P('chan'), may hold values from 0.25 to 1.75
- merge_shift: float32 [256], P('chan'), may hold values from -3 to 3
Outputs:
- merged: bfloat16 [48, 256, 256], P(None, 'lon', 'chan')
The draws below stay inside these ranges and needn't reach their ends.
All inputs are finite; a program needn't handle non-finite values.
Results may differ from the reference program's by a relative error of at most 0.0065.
Values may be sent and summed in bfloat16 or wider, within the bound.
A program may use at most 64 MiB of HBM per device.

```python
import jax
import jax.numpy as jnp
from jax import lax

CHANNELS = 2048
BRANCH = 256
SKIPS = 48
ROWS = 48
LON_DEV = 8
LONS = 256


def draw_features(key, part):
    key = jax.random.fold_in(key, 7)
    key_mean, key_noise, key_block = jax.random.split(key, 3)
    channel_mean = jax.random.uniform(key_mean, (CHANNELS,), jnp.float32, -1.5, 1.5)
    ramp = 0.5 + jnp.arange(LONS, dtype=jnp.float32) / (LONS - 1)
    block_offset = jax.random.uniform(key_block, (LONS // LON_DEV, CHANNELS), jnp.float32, -2.0, 2.0)
    block_field = jnp.repeat(block_offset, LON_DEV, axis=0)
    noise = jnp.clip(jax.random.normal(key_noise, (ROWS, LONS, CHANNELS), jnp.float32), -5.0, 5.0)
    total = noise + ramp[None, :, None] * channel_mean[None, None, :] + block_field[None, :, :]
    return jnp.clip(total, -6.0, 6.0).astype(jnp.bfloat16)


def steps_of(stream_key, dims, cuts, low, top_value):
    factor_of = 1.0
    for position, parts in cuts:
        steps = jax.random.uniform(jax.random.fold_in(jax.random.fold_in(stream_key, 6), position), (parts,), jnp.float32, low / len(cuts), top_value / len(cuts))
        factor_of = factor_of * jnp.repeat(jnp.exp(steps), dims[position] // parts).reshape((-1,) + (1,) * (len(dims) - 1 - position))
    return factor_of


def centred(stream_key, shape, deviation, limit, cuts=(), held_as=jnp.bfloat16):
    gain = steps_of(stream_key, shape, cuts, -0.22, 0.18) if cuts else 1.0
    values = jax.random.normal(stream_key, shape, jnp.float32) * deviation * gain
    return jnp.minimum(jnp.maximum(values, -limit), limit).astype(held_as)


def setup_inputs(seed: int = 0) -> dict:
    keys = jax.random.split(jax.random.key(seed), 14)
    return {
        "features": draw_features(jax.random.fold_in(keys[13], 71), 0),
        "w_point": centred(keys[1], (CHANNELS, BRANCH), CHANNELS ** -0.5, 0.125, ((0, 16),)),
        "w_dilated": centred(keys[2], (3, 3, 3, CHANNELS, BRANCH), (9 * CHANNELS) ** -0.5, 0.046875, ((3, 16),)),
        "w_pool": centred(keys[3], (CHANNELS, BRANCH), CHANNELS ** -0.5, 0.125, ((0, 16),)),
        "bn_scale": jnp.clip(1.0 + 0.15 * jax.random.normal(keys[4], (5, BRANCH), jnp.float32), 0.25, 1.75),
        "bn_shift": centred(keys[5], (5, BRANCH), 0.5, 3.0, (), jnp.float32),
        "proj_weight": centred(keys[6], (5, BRANCH, BRANCH), (5 * BRANCH) ** -0.5, 0.15625, ((2, 16),)),
        "proj_scale": jnp.clip(1.0 + 0.15 * jax.random.normal(keys[7], (BRANCH,), jnp.float32), 0.25, 1.75),
        "proj_shift": centred(keys[8], (BRANCH,), 0.5, 3.0, ((0, 16),), jnp.float32),
        "skip": centred(keys[9], (ROWS, LONS, SKIPS), 1.0, 6.0, ((1, 32),)),
        "merge_weight": centred(keys[10], (3, 3, BRANCH + SKIPS, BRANCH), (9 * (BRANCH + SKIPS)) ** -0.5, 0.109375, ((3, 16),)),
        "merge_scale": jnp.clip(1.0 + 0.15 * jax.random.normal(keys[11], (BRANCH,), jnp.float32), 0.25, 1.75),
        "merge_shift": centred(keys[12], (BRANCH,), 0.5, 3.0, ((0, 16),), jnp.float32),
    }


dilations = (12, 24, 36)


def wrap_pad(field, margin):
    col_total = field.shape[1]
    columns = (jnp.arange(col_total + 2 * margin) - margin) % col_total
    wrapped = jnp.take(field, columns.astype(jnp.int32), axis=1)
    return jnp.pad(wrapped, ((margin, margin), (0, 0), (0, 0)))


def tap_sum(padded, weights, dilation, margin, out_rows, out_cols):
    running = jnp.zeros((out_rows * out_cols, weights.shape[-1]), jnp.float32)
    for tap_row in range(3):
        for tap_col in range(3):
            top = margin + (tap_row - 1) * dilation
            left = margin + (tap_col - 1) * dilation
            window = padded[top:top + out_rows, left:left + out_cols]
            running = running + jnp.dot(window.reshape(out_rows * out_cols, -1), weights[tap_row, tap_col], preferred_element_type=jnp.float32)
    return running


def reference(features, w_point, w_dilated, w_pool, bn_scale, bn_shift, proj_weight, proj_scale, proj_shift, skip, merge_weight, merge_scale, merge_shift):
    rim_width = max(dilations)
    cell_count = ROWS * LONS
    flat = features.reshape(cell_count, CHANNELS)
    outputs = [jnp.dot(flat, w_point, preferred_element_type=jnp.float32)]
    padded = wrap_pad(features, rim_width)
    for rate_index, dilation in enumerate(dilations):
        outputs.append(tap_sum(padded, w_dilated[rate_index], dilation, rim_width, ROWS, LONS))
    channel_sums = jnp.sum(flat, axis=0, dtype=jnp.float32).reshape(1, CHANNELS)
    image = jnp.dot(channel_sums, w_pool.astype(jnp.float32), precision=lax.Precision.HIGHEST) / (ROWS * LONS)
    outputs.append(jnp.broadcast_to(image, (cell_count, BRANCH)))
    branches = jnp.stack(outputs, axis=1)
    activated = jax.nn.relu(branches * bn_scale + bn_shift).astype(jnp.bfloat16)
    projected = jnp.dot(activated.reshape(cell_count, 5 * BRANCH), proj_weight.reshape(5 * BRANCH, BRANCH), preferred_element_type=jnp.float32)
    pooled = jax.nn.relu(projected * proj_scale + proj_shift).astype(jnp.bfloat16).reshape(ROWS, LONS, BRANCH)
    joined = jnp.concatenate([pooled, skip], axis=2)
    mixed = tap_sum(wrap_pad(joined, 1), merge_weight, 1, 1, ROWS, LONS)
    return jax.nn.relu(mixed * merge_scale + merge_shift).astype(jnp.bfloat16).reshape(ROWS, LONS, BRANCH)
```

```python
import functools

import jax
import jax.numpy as jnp
from jax import lax
from jax.experimental import pallas as pl
from jax.experimental.pallas import tpu as pltpu
from jax.sharding import PartitionSpec as P

BF = jnp.bfloat16
F32 = jnp.float32
MESH = pl.DeviceIdType.MESH

ROWS, COLS, CH, BR, SK = 48, 8, 128, 256, 48
OWN = 3
RIM = 36
RATES = (2, 1, 0)
DIL = (12, 24, 36)
ORDERS = ((0, 2, 1), (2, 1, 0), (1, 0, 2))
LANES = ((0, 512), (512, 896), (896, 1280))
FAR = ((2, 1), (3, 3), (5, 4))
GRAY = ((0, 0), (0, 1), (1, 1), (1, 0))


def dot(a, b):
    return lax.dot_general(a, b, (((1,), (0,)), ((), ())), preferred_element_type=F32)


def dot_nt(a, b):
    return lax.dot_general(a, b, (((1,), (1,)), ((), ())), preferred_element_type=F32)


def to_tiles(v):
    n = v.shape[0] // 8
    lo = v[:, :128].reshape(n, 8, 128)
    hi = v[:, 128:].reshape(n, 8, 128)
    return jnp.concatenate([lo, hi], axis=1)


def from_tiles(t):
    n = t.shape[0]
    lo = t[:, :8].reshape(n * 8, 128)
    hi = t[:, 8:].reshape(n * 8, 128)
    return jnp.concatenate([lo, hi], axis=1)


class Several:
    def __init__(self):
        self.copies = []

    def wait(self):
        for cp in self.copies:
            cp.wait()


def kernel(
    n_lon,
    feat_h, wpt_h, wd_h, wpool_h, bns_h, bnt_h, pw_h, ps_h, pt_h, skip_h, mw_h, ms_h, mt_h,
    out_ref,
    feat, wpt, wd, wpool, bns, bnt, ps, pt, skip, ms, mt,
    xpad,
    acc0, sb0, r0, acc1, sb1, r1, acc2, sb2, r2, acc3, sb3, r3,
    pacc0, psb0, pr0, pacc1, psb1, pr1, pacc2, psb2, pr2, pacc3, psb3, pr3,
    fin, sh, rsh,
    wt0, wt1, wt2,
    ia, ib, ic, img,
    gat, wrow, wcat, vskip, proj, ev, rev,
    ld_sem, pw_sem, mw_sem,
    rs_s, rs_r, sh_s, sh_r, wt_s, wt_r, ia_s, ia_r, ib_s, ib_r, ic_s, ic_r, ga_s, ga_r, ev_s, ev_r,
):
    lon = lax.axis_index("lon")
    chan = lax.axis_index("chan")
    a = chan // 8
    y = (chan // 2) % 4
    c = chan % 2
    bit = (a, y // 2, (y % 2 + y // 2) % 2)
    beta = c * 8 + bit[0] * 4 + bit[1] * 2 + bit[2]

    loads = {}
    for i, (name, src, dst) in enumerate(
        [
            ("feat", feat_h, feat), ("wd2", wd_h.at[2], wd.at[2]), ("wd1", wd_h.at[1], wd.at[1]),
            ("wd0", wd_h.at[0], wd.at[0]), ("wpt", wpt_h, wpt), ("wpool", wpool_h, wpool),
            ("ps", ps_h, ps), ("pt", pt_h, pt), ("bns", bns_h, bns), ("bnt", bnt_h, bnt), ("skip", skip_h, skip),
            ("ms", ms_h, ms), ("mt", mt_h, mt),
        ]
    ):
        loads[name] = pltpu.make_async_copy(src, dst, ld_sem.at[i])
        loads[name].start()

    for p, ((s, e), ref) in enumerate(zip(LANES, (wt0, wt1, wt2))):
        loads[f"wt{p}"] = Several()
        for b in range(5):
            lo, hi = max(b * BR, s), min(b * BR + BR, e)
            if lo < hi:
                cp = pltpu.make_async_copy(
                    pw_h.at[b, :, lo - b * BR : hi - b * BR],
                    ref.at[bit[0], bit[1], bit[2], c, :, lo - s : hi - s],
                    pw_sem.at[p, b],
                )
                cp.start()
                loads[f"wt{p}"].copies.append(cp)
    loads["mw"] = Several()
    for t in range(3):
        for b in range(3):
            cp = pltpu.make_async_copy(mw_h.at[t, b], wrow.at[t, 16 * b : 16 * b + 16], mw_sem.at[t, b])
            cp.start()
            loads["mw"].copies.append(cp)

    def chan_peer(m):
        mc, mx, mh, ml = (m >> 3) & 1, (m >> 2) & 1, (m >> 1) & 1, m & 1
        pc = 1 - c if mc else c
        pa = 1 - a if mx else a
        flip = y + 1 - 2 * (y % 2)
        py = {(0, 0): y, (0, 1): flip, (1, 0): 3 - y, (1, 1): (y + 2) % 4}[(mh, ml)]
        return (lon, pa * 8 + py * 2 + pc)

    def beta_peer(m):
        bits = [c, *bit]
        masks = [(m >> 3) & 1, (m >> 2) & 1, (m >> 1) & 1, m & 1]
        f = [1 - b if k else b for b, k in zip(bits, masks)]
        return f[0] * 8 + f[1] * 4 + f[2] * 2 + f[3]

    sibling = chan_peer(8)
    step_peer = (chan_peer(4), chan_peer(2), chan_peer(1))

    def lon_peer(k):
        return ((lon + k + n_lon) % n_lon, chan)

    def lon_xor(m):
        out = lon
        for p in range(5):
            if (m >> p) & 1:
                b = (lon // (1 << p)) % 2
                out = out + (1 - 2 * b) * (1 << p)
        return (out, chan)

    near = list(range(1, 8))
    wide = [8 * m for m in range(1, n_lon // 8)]

    barrier = pltpu.get_barrier_semaphore()
    greeted = 0
    for dev in (
        [chan_peer(m) for m in range(1, 16)]
        + [lon_peer(k) for k in (1, 2, 3, 4, 5, -1, -2, -3, -4, -5)]
        + [lon_xor(m) for m in near + wide]
    ):
        pl.semaphore_signal(barrier, inc=1, device_id=dev, device_id_type=MESH)
        greeted += 1

    sends = []

    def send(src, dst, s, r, dev):
        cp = pltpu.make_async_remote_copy(
            src_ref=src, dst_ref=dst, send_sem=s, recv_sem=r, device_id=dev, device_id_type=MESH
        )
        cp.start()
        sends.append(cp)
        return cp

    A0, SB0, R0 = [acc0.at[0], acc0.at[1], acc0.at[2], pacc0], [sb0.at[0], sb0.at[1], sb0.at[2], psb0], [r0.at[0], r0.at[1], r0.at[2], pr0]
    ACC = [[acc1.at[k] for k in range(3)] + [pacc1], [acc2.at[k] for k in range(3)] + [pacc2], [acc3.at[k] for k in range(3)] + [pacc3]]
    SB = [[sb1.at[k] for k in range(3)] + [psb1], [sb2.at[k] for k in range(3)] + [psb2], [sb3.at[k] for k in range(3)] + [psb3]]
    RR = [[r1.at[k] for k in range(3)] + [pr1], [r2.at[k] for k in range(3)] + [pr2], [r3.at[k] for k in range(3)] + [pr3]]

    def put(k, p, tiles):
        t = tiles.reshape((2, 2, 2, 2) + tiles.shape[1:])
        A0[k][p] = t
        SB0[k][p] = t.astype(BF)

    def compute(k):
        if k < 3:
            rate = RATES[k]
            d = DIL[rate]
            loads[f"wd{rate}"].wait()
            lhs = jnp.concatenate(
                [xpad[(RIM + (t - 1) * d) * 8 : (RIM + (t - 1) * d + ROWS) * 8] for t in range(3)], axis=1
            )
            for tap in range(3):
                rhs = wd[rate, :, tap].reshape(3 * CH, BR)
                res = to_tiles(dot(lhs, rhs))
                put(k, tap, res.reshape(16, OWN, 16, 128))
        else:
            loads["wpt"].wait()
            res = to_tiles(dot(xpad[RIM * 8 : (RIM + ROWS) * 8], wpt[...])).reshape(16, OWN, 16, 128)
            for p in range(3):
                put(k, p, res[:, p : p + 1])

    pending = {}

    def core_send(k):
        pending[k, 0] = [
            send(SB0[k].at[p, 1 - c], R0[k].at[p], rs_s.at[k, 0, p], rs_r.at[k, 0, p], sibling) for p in range(3)
        ]

    def halve(k, step):
        sent = pending.pop((k, step))
        out = []
        for p in range(3):
            sent[p].wait_recv()
            left = [d for d in (0, 1, 2) if d not in ORDERS[p][:step]]
            mine = A0[k].at[p, c] if step == 0 else ACC[step - 1][k].at[p]
            got = R0[k].at[p] if step == 0 else RR[step - 1][k].at[p]
            d = ORDERS[p][step]

            def half(v):
                return tuple(v if q == d else slice(None) for q in left)

            there, here = half(1 - bit[d]), half(bit[d])
            shape = SB[step][k].shape[1:]
            SB[step][k][p] = (mine[there] + got[there].astype(F32)).astype(BF).reshape(shape)
            out.append(
                send(SB[step][k].at[p], RR[step][k].at[p], rs_s.at[k, step + 1, p], rs_r.at[k, step + 1, p], step_peer[d])
            )
            ACC[step][k][p] = (mine[here] + got[here].astype(F32)).reshape(shape)
        pending[k, step + 1] = out

    shifts = {}

    def finish(k):
        sent = pending.pop((k, 3))
        for p in (0, 2, 1):
            sent[p].wait_recv()
            v = ACC[2][k][p] + RR[2][k][p].astype(F32)
            if k == 3:
                fin[3, p : p + 1] = v
                continue
            if p == 1:
                fin[k] = v
                continue
            side, sign = (0, 1) if p == 0 else (1, -1)
            sh[k, side] = v.astype(BF)
            first, second = FAR[RATES[k]]
            if p == 2:
                first, second = second, first
            for j, dist in enumerate((first,) if first == second else (first, second)):
                shifts[k, side, j] = send(
                    sh.at[k, side], rsh.at[k, side, j], sh_s.at[k, side, j], sh_r.at[k, side, j], lon_peer(sign * dist)
                )

    def weights(l0, l1):
        parts = []
        for (s, e), ref in zip(LANES, (wt0, wt1, wt2)):
            lo, hi = max(l0, s), min(l1, e)
            if lo < hi:
                parts.append(
                    jnp.concatenate(
                        [ref[q, GRAY[v][0], GRAY[v][1], w, :, lo - s : hi - s] for q in (0, 1) for v in range(4) for w in (0, 1)],
                        axis=0,
                    )
                )
        return parts[0] if len(parts) == 1 else jnp.concatenate(parts, axis=1)

    def project(branch, value):
        act = jnp.maximum(value * bns[branch : branch + 1] + bnt[branch : branch + 1], 0.0)
        return dot_nt(act.astype(BF), weights(branch * BR, branch * BR + BR))

    def pad32(v):
        return jnp.concatenate([v, jnp.zeros((8, BR), F32)], axis=0)

    def branch_of(k):
        col = lax.broadcasted_iota(jnp.int32, (2 * OWN, 8, 128), 1)
        total = fin[k]
        for side in (0, 1):
            count = 1 if RATES[k] == 1 else 2
            tiles = []
            for j in range(count):
                shifts[k, side, j].wait_recv()
                tiles.append(rsh[k, side, j].astype(F32).reshape(2 * OWN, 8, 128))
            if count == 1:
                moved = tiles[0]
            else:
                moved = pltpu.roll(jnp.where(col >= 4, tiles[0], tiles[1]), 4, 1)
            total = total + moved.reshape(OWN, 16, 128)
        return project(1 + RATES[k], pad32(from_tiles(total)))

    WT = (wt0, wt1, wt2)
    wsent = {}

    def wt_step(step):
        for p in range(3):
            if step:
                wsent[step - 1, p].wait_recv()
            else:
                loads[f"wt{p}"].wait()
            done = ORDERS[p][:step]
            idx = tuple(slice(None) if d in done else bit[d] for d in range(3)) + (c,)
            ref = WT[p].at[idx]
            wsent[step, p] = send(ref, ref, wt_s.at[step, p], wt_r.at[step, p], step_peer[ORDERS[p][step]])

    def wt_core():
        for p in range(3):
            wsent[2, p].wait_recv()
            ref = WT[p].at[:, :, :, c]
            wsent[3, p] = send(ref, ref, wt_s.at[3, p], wt_r.at[3, p], sibling)

    isent = {}

    def image_start():
        loads["wpool"].wait()
        sums = jnp.sum(feat[...].astype(F32).reshape(ROWS * COLS, CH), axis=0, keepdims=True)
        hi = sums.astype(BF)
        rest = sums - hi.astype(F32)
        mid = rest.astype(BF)
        low = (rest - mid.astype(F32)).astype(BF)
        row = lax.broadcasted_iota(jnp.int32, (16, CH), 0)
        lhs = jnp.where(
            row == 0,
            hi.astype(F32),
            jnp.where(row == 1, mid.astype(F32), jnp.where(row == 2, low.astype(F32), 0.0)),
        ).astype(BF)
        ia[0] = jnp.sum(dot(lhs, wpool[...]), axis=0, keepdims=True)
        for m in near:
            isent[0, m] = send(ia.at[0], ia.at[m], ia_s.at[m], ia_r.at[m], lon_xor(m))

    def image_wide():
        for m in near:
            isent[0, m].wait_recv()
        total = ia[0]
        for m in near:
            total = total + ia[m]
        ib[0] = total
        for m in wide:
            isent[1, m] = send(ib.at[0], ib.at[m // 8], ib_s.at[m // 8], ib_r.at[m // 8], lon_xor(m))

    def image_chan():
        total = ib[0]
        for m in wide:
            isent[1, m].wait_recv()
            total = total + ib[m // 8]
        total = total / (ROWS * COLS * n_lon)
        loads["ps"].wait()
        loads["pt"].wait()
        lane = lax.broadcasted_iota(jnp.int32, (1, BR), 1) - chan * 16
        scale = jnp.zeros((1, BR), F32)
        shift = jnp.zeros((1, BR), F32)
        for i in range(16):
            scale = jnp.where(lane == i, ps[i], scale)
            shift = jnp.where(lane == i, pt[i], shift)
        ic[0, 0] = total
        ic[0, 1] = scale
        ic[0, 2] = shift
        for m in range(1, 16):
            isent[2, m] = send(ic.at[0], ic.at[m], ic_s.at[m], ic_r.at[m], chan_peer(m))

    def image_end():
        for m in range(1, 16):
            isent[2, m].wait_recv()
        total = ic[0]
        for m in range(1, 16):
            total = total + ic[m]
        img[...] = total

    def merge_prepare():
        loads["mw"].wait()
        loads["skip"].wait()
        wide_rows = (BR + SK, BR + SK)
        eye = (
            lax.broadcasted_iota(jnp.int32, wide_rows, 0) == lax.broadcasted_iota(jnp.int32, wide_rows, 1)
        ).astype(BF)
        for t in range(3):
            wrow[t, 48:] = jnp.zeros((80, BR + SK), BF)
            wcat[t] = dot_nt(eye, wrow[t]).astype(BF)
        s2 = skip[...].astype(F32).reshape(ROWS * COLS, SK).astype(BF)
        vskip[...] = rows_shifted([dot(s2, wcat[t, BR:]) for t in range(3)])

    def rows_shifted(parts):
        zero = jnp.zeros((8, 128), F32)
        n = ROWS * COLS
        up = jnp.concatenate([zero, parts[0][: n - 8]], axis=0)
        down = jnp.concatenate([parts[2][8:], zero], axis=0)
        return parts[1] + up + down

    loads["feat"].wait()
    x2 = feat[...].astype(F32).reshape(ROWS * COLS, CH).astype(BF)
    xpad[: RIM * 8] = jnp.zeros((RIM * 8, CH), BF)
    xpad[(RIM + ROWS) * 8 :] = jnp.zeros((RIM * 8, CH), BF)
    xpad[RIM * 8 : (RIM + ROWS) * 8] = x2
    compute(0)
    pl.semaphore_wait(barrier, greeted)
    core_send(0)
    compute(1)
    core_send(1)
    halve(0, 0)
    image_start()
    compute(2)
    core_send(2)
    halve(1, 0)
    wt_step(0)
    compute(3)
    core_send(3)
    halve(0, 1)
    halve(2, 0)
    image_wide()
    halve(1, 1)
    halve(3, 0)
    wt_step(1)
    halve(0, 2)
    image_chan()
    halve(2, 1)
    halve(3, 1)
    halve(1, 2)
    wt_step(2)
    merge_prepare()
    finish(0)
    halve(2, 2)
    halve(3, 2)
    finish(1)
    wt_core()
    finish(2)
    image_end()
    loads["bns"].wait()
    loads["bnt"].wait()
    for p in range(3):
        wsent[3, p].wait_recv()
    proj[...] = branch_of(0)
    proj[...] += project(4, jnp.broadcast_to(img[0], (32, BR)))
    proj[...] += branch_of(1)
    finish(3)
    proj[...] += project(0, pad32(from_tiles(fin[3])))
    pooled = proj[...] + branch_of(2)
    pooled = jnp.maximum(pooled * img[1] + img[2], 0.0)[: OWN * 8]
    gat[beta] = to_tiles(pooled).astype(BF)
    gsent = [send(gat.at[beta], gat.at[beta], ga_s.at[m], ga_r.at[m], chan_peer(m)) for m in range(1, 16)]
    for g in gsent:
        g.wait_recv()
    pf = from_tiles(gat[...].astype(F32).reshape(ROWS, 16, 128)).astype(BF)
    v = vskip[...] + rows_shifted([dot(pf, wcat[t, :BR]) for t in range(3)])
    vb = v.astype(BF)
    pick_r = lax.broadcasted_iota(jnp.int32, (ROWS, ROWS * COLS), 0)
    pick_c = lax.broadcasted_iota(jnp.int32, (ROWS, ROWS * COLS), 1)
    esent = []
    for i, (col, k) in enumerate(((7, 1), (0, -1))):
        ev[i] = dot((pick_c == pick_r * 8 + col).astype(BF), vb).astype(BF)
        esent.append(send(ev.at[i], rev.at[i], ev_s.at[i], ev_r.at[i], lon_peer(k)))
    v3 = v.reshape(ROWS, 8, 128)
    col = lax.broadcasted_iota(jnp.int32, (ROWS, 8, 128), 1)
    mid = pltpu.roll(v3, 112, 2)
    left = jnp.where(col == 0, 0.0, pltpu.roll(v3, 1, 1))
    right = jnp.where(col == 7, 0.0, pltpu.roll(pltpu.roll(v3, 96, 2), 7, 1))
    total = mid + left + right
    spread_r = lax.broadcasted_iota(jnp.int32, (ROWS * COLS, ROWS), 0)
    spread_c = lax.broadcasted_iota(jnp.int32, (ROWS * COLS, ROWS), 1)
    esent[0].wait_recv()
    esent[1].wait_recv()
    west = dot((spread_r == spread_c * 8).astype(BF), rev[0])
    east = dot((spread_r == spread_c * 8 + 7).astype(BF), rev[1])
    total = total + west.reshape(ROWS, 8, 128) + pltpu.roll(east.reshape(ROWS, 8, 128), 96, 2)
    loads["ms"].wait()
    loads["mt"].wait()
    lane = lax.broadcasted_iota(jnp.int32, (1, 1, 128), 2)
    scale = jnp.zeros((1, 1, 128), F32)
    shift = jnp.zeros((1, 1, 128), F32)
    for i in range(16):
        scale = jnp.where(lane == i, ms[i], scale)
        shift = jnp.where(lane == i, mt[i], shift)
    out_ref[...] = jnp.maximum(total * scale + shift, 0.0)[:, :, :16].astype(BF)
    for cp in sends:
        cp.wait_send()


def body(features, w_point, w_dilated, w_pool, bn_scale, bn_shift, proj_weight, proj_scale, proj_shift, skip, merge_weight, merge_scale, merge_shift):
    n_lon = lax.axis_size("lon")
    vm = pltpu.VMEM
    dma = pltpu.SemaphoreType.DMA
    t3, t1 = (OWN, 16, 128), (1, 16, 128)

    def steps(lead, t):
        shapes = [
            vm(lead + (3, 2, 2, 2, 2) + t, F32), vm(lead + (3, 2, 2, 2, 2) + t, BF), vm(lead + (3, 2, 2, 2) + t, BF),
        ]
        for rest in ((2, 2), (2,), ()):
            shapes += [vm(lead + (3,) + rest + t, F32), vm(lead + (3,) + rest + t, BF), vm(lead + (3,) + rest + t, BF)]
        return shapes

    scratch = (
        [
            vm((ROWS, COLS, CH), BF), vm((CH, BR), BF), vm((3, 3, 3, CH, BR), BF), vm((CH, BR), BF),
            vm((5, BR), F32), vm((5, BR), F32), pltpu.SMEM((16,), F32), pltpu.SMEM((16,), F32),
            vm((ROWS, COLS, SK), BF), pltpu.SMEM((16,), F32), pltpu.SMEM((16,), F32),
            vm(((ROWS + 2 * RIM) * 8, CH), BF),
        ]
        + steps((3,), t3)
        + steps((), t1)
        + [
            vm((4,) + t3, F32), vm((3, 2) + t3, BF), vm((3, 2, 2) + t3, BF),
            vm((2, 2, 2, 2, 16, 512), BF), vm((2, 2, 2, 2, 16, 384), BF), vm((2, 2, 2, 2, 16, 384), BF),
            vm((8, 1, BR), F32), vm((4, 1, BR), F32), vm((16, 3, 1, BR), F32), vm((3, 1, BR), F32),
            vm((16,) + t3, BF), vm((3, 128, BR + SK), BF), vm((3, BR + SK, 128), BF), vm((ROWS * COLS, 128), F32), vm((32, BR), F32),
            vm((2, ROWS, 128), BF), vm((2, ROWS, 128), BF),
            dma((13,)), dma((3, 5)), dma((3, 3)),
            dma((4, 4, 3)), dma((4, 4, 3)), dma((3, 2, 2)), dma((3, 2, 2)), dma((4, 3)), dma((4, 3)),
            dma((8,)), dma((8,)), dma((4,)), dma((4,)), dma((16,)), dma((16,)), dma((16,)), dma((16,)), dma((2,)), dma((2,)),
        ]
    )
    return pl.pallas_call(
        functools.partial(kernel, n_lon),
        out_shape=jax.ShapeDtypeStruct((ROWS, COLS, 16), BF),
        in_specs=[pl.BlockSpec(memory_space=pltpu.HBM)] * 13,
        out_specs=pl.BlockSpec(memory_space=pltpu.VMEM),
        scratch_shapes=scratch,
        compiler_params=pltpu.CompilerParams(
            collective_id=0, has_side_effects=True, vmem_limit_bytes=48 * 1024 * 1024
        ),
        name="aspp_head",
    )(features, w_point, w_dilated, w_pool, bn_scale, bn_shift, jnp.swapaxes(proj_weight, 1, 2), proj_scale, proj_shift, skip, jnp.swapaxes(merge_weight, 2, 3), merge_scale, merge_shift)


def solution(mesh):
    return jax.shard_map(
        body,
        mesh=mesh,
        in_specs=(
            P(None, "lon", "chan"),
            P("chan", None),
            P(None, None, None, "chan", None),
            P("chan", None),
            P(),
            P(),
            P(None, None, "chan"),
            P("chan"),
            P("chan"),
            P(None, "lon", None),
            P(None, None, None, "chan"),
            P("chan"),
            P("chan"),
        ),
        out_specs=P(None, "lon", "chan"),
        check_vma=False,
    )
```

```python
import functools

import jax
import jax.numpy as jnp
from jax import lax
from jax.experimental import pallas as pl
from jax.experimental.pallas import tpu as pltpu
from jax.sharding import PartitionSpec as P

BF = jnp.bfloat16
F32 = jnp.float32
MESH = pl.DeviceIdType.MESH

ROWS, COLS, CH, BR, SK = 48, 8, 128, 256, 48
OWN = 3
RIM = 36
DIL = (12, 24, 36)
CHUNKS = (
    ((((2, 0), 0, 3),), (((2, 2), 0, 3),), (((1, 0), 0, 3),)),
    ((((1, 2), 0, 3),), (((0, 0), 0, 3),), (((0, 2), 0, 3),)),
    (
        (((2, 1), 0, 4), ("point", 0, 2)),
        (((1, 1), 0, 4), ("point", 2, 3)),
        (((0, 1), 0, 4), ("point", 3, 4)),
    ),
)
TILES = [[sum(hi - lo for _, lo, hi in part) for part in chunk] for chunk in CHUNKS]
ORDERS = ((0, 2, 1), (2, 1, 0), (1, 0, 2))
LANES = ((0, 512), (512, 896), (896, 1280))
FAR = {(0, 0): (2, 1), (0, 2): (1, 2), (1, 0): (3, 4, 2), (1, 2): (3, 2, 4), (2, 0): (5, 4), (2, 2): (4, 5)}
GRAY = ((0, 0), (0, 1), (1, 1), (1, 0))


def dot(a, b):
    return lax.dot_general(a, b, (((1,), (0,)), ((), ())), preferred_element_type=F32)


def dot_nt(a, b):
    return lax.dot_general(a, b, (((1,), (1,)), ((), ())), preferred_element_type=F32)


def to_tiles(v):
    n = v.shape[0] // 8
    lo = v[:, :128].reshape(n, 8, 128)
    hi = v[:, 128:].reshape(n, 8, 128)
    return jnp.concatenate([lo, hi], axis=1)


def from_tiles(t):
    n = t.shape[0]
    lo = t[:, :8].reshape(n * 8, 128)
    hi = t[:, 8:].reshape(n * 8, 128)
    return jnp.concatenate([lo, hi], axis=1)


class Several:
    def __init__(self):
        self.copies = []

    def wait(self):
        for cp in self.copies:
            cp.wait()


def kernel(
    n_lon,
    feat_h, wpt_h, wd_h, wpool_h, bns_h, bnt_h, pw_h, ps_h, pt_h, skip_h, mw_h, ms_h, mt_h,
    out_ref,
    *refs,
):
    (feat, wpt, wd, wpool, bns, bnt, ps, pt, skip, ms, mt, xs, xpad, hpad, edge, hedge), refs = refs[:16], refs[16:]
    steps, refs = refs[:108], refs[108:]
    (
        fin, sh, rsh, wt0, wt1, wt2, ia, ib, ic, img, gat, wrow, wcat, vskip, vskip_out, proj,
        ld_sem, pw_sem, mw_sem, known,
        rs_s, rs_r, sh_s, sh_r, wt_s, wt_r, ia_s, ia_r, ib_s, ib_r, ic_s, ic_r, ga_s, ga_r, ev_s, ev_r,
    ) = refs
    A0, SB0, R0 = ([[steps[(k * 3 + p) * 12 + i] for p in range(3)] for k in range(3)] for i in range(3))
    ACC, SB, RR = (
        [[[steps[(k * 3 + p) * 12 + 3 * (q + 1) + i] for p in range(3)] for k in range(3)] for q in range(3)] for i in range(3)
    )
    lon = lax.axis_index("lon")
    chan = lax.axis_index("chan")
    a = chan // 8
    y = (chan // 2) % 4
    c = chan % 2
    bit = (a, y // 2, (y % 2 + y // 2) % 2)
    beta = c * 8 + bit[0] * 4 + bit[1] * 2 + bit[2]

    loads = {}
    for i, (name, src, dst) in enumerate(
        [
            ("feat", feat_h, feat), ("wd2", wd_h.at[2], wd.at[2]), ("wd1", wd_h.at[1], wd.at[1]),
            ("wd0", wd_h.at[0], wd.at[0]), ("wpt", wpt_h, wpt), ("wpool", wpool_h, wpool),
            ("ps", ps_h, ps), ("pt", pt_h, pt), ("bns", bns_h, bns), ("bnt", bnt_h, bnt), ("skip", skip_h, skip),
            ("ms", ms_h, ms), ("mt", mt_h, mt),
        ]
    ):
        loads[name] = pltpu.make_async_copy(src, dst, ld_sem.at[i])
        loads[name].start()

    for p, ((s, e), ref) in enumerate(zip(LANES, (wt0, wt1, wt2))):
        loads[f"wt{p}"] = Several()
        for b in range(5):
            lo, hi = max(b * BR, s), min(b * BR + BR, e)
            if lo < hi:
                cp = pltpu.make_async_copy(
                    pw_h.at[b, :, lo - b * BR : hi - b * BR],
                    ref.at[bit[0], bit[1], bit[2], c, :, lo - s : hi - s],
                    pw_sem.at[p, b],
                )
                cp.start()
                loads[f"wt{p}"].copies.append(cp)
    loads["mw"] = Several()
    for t in range(3):
        for b in range(3):
            cp = pltpu.make_async_copy(mw_h.at[t, b], wrow.at[t, 16 * b : 16 * b + 16], mw_sem.at[t, b])
            cp.start()
            loads["mw"].copies.append(cp)

    def chan_peer(m):
        mc, mx, mh, ml = (m >> 3) & 1, (m >> 2) & 1, (m >> 1) & 1, m & 1
        pc = 1 - c if mc else c
        pa = 1 - a if mx else a
        flip = y + 1 - 2 * (y % 2)
        py = {(0, 0): y, (0, 1): flip, (1, 0): 3 - y, (1, 1): (y + 2) % 4}[(mh, ml)]
        return (lon, pa * 8 + py * 2 + pc)

    def beta_peer(m):
        bits = [c, *bit]
        masks = [(m >> 3) & 1, (m >> 2) & 1, (m >> 1) & 1, m & 1]
        f = [1 - b if k else b for b, k in zip(bits, masks)]
        return f[0] * 8 + f[1] * 4 + f[2] * 2 + f[3]

    sibling = chan_peer(8)
    step_peer = (chan_peer(4), chan_peer(2), chan_peer(1))

    def lon_peer(k):
        return ((lon + k + n_lon) % n_lon, chan)

    def lon_xor(m):
        out = lon
        for p in range(5):
            if (m >> p) & 1:
                b = (lon // (1 << p)) % 2
                out = out + (1 - 2 * b) * (1 << p)
        return (out, chan)

    near = list(range(1, 8))
    blocks = n_lon // 8

    barrier = pltpu.get_barrier_semaphore()
    greeted = 0
    for dev in (
        [chan_peer(m) for m in range(1, 16)]
        + [lon_peer(k) for k in (1, 2, 3, 4, 5, -1, -2, -3, -4, -5)]
        + [lon_xor(m) for m in near]
        + ([lon_peer(8), lon_peer(-8)] if blocks > 1 else [])
    ):
        pl.semaphore_signal(barrier, inc=1, device_id=dev, device_id_type=MESH)
        greeted += 1

    sends = []

    def send(src, dst, s, r, dev):
        cp = pltpu.make_async_remote_copy(
            src_ref=src, dst_ref=dst, send_sem=s, recv_sem=r, device_id=dev, device_id_type=MESH
        )
        cp.start()
        sends.append(cp)
        return cp

    def taps(ref, d):
        return jnp.concatenate([ref[(RIM + (t - 1) * d) * 8 : (RIM + (t - 1) * d + ROWS) * 8] for t in range(3)], axis=1)

    def field(which, ref):
        if which == "point":
            return to_tiles(dot(ref[RIM * 8 : (RIM + ROWS) * 8], wpt[...])).reshape(16, OWN, 16, 128)
        rate, tap = which
        res = dot(taps(ref, DIL[rate]), wd[rate, :, tap].reshape(3 * CH, BR))
        return to_tiles(res).reshape(16, OWN, 16, 128)

    def whole(which, outer):
        main = field(which, xpad)
        if not outer:
            return main
        rim = field(which, hpad).reshape(16, OWN, 2, 8, 128)
        last = rim[:, 0] + sum(
            pltpu.roll(rim[:, j].reshape(32, 8, 128), 2 * j, 1).reshape(16, 2, 8, 128) for j in range(1, OWN)
        )
        return jnp.concatenate([main, last.reshape(16, 1, 16, 128)], axis=1)

    def compute(k):
        made = {}
        for p in range(3):
            at = 0
            for which, lo, hi in CHUNKS[k][p]:
                if which not in made:
                    made[which] = whole(which, k == 2)
                t = made[which][:, lo:hi].reshape(2, 2, 2, 2, hi - lo, 16, 128)
                A0[k][p][:, :, :, :, at : at + hi - lo] = t
                SB0[k][p][:, :, :, :, at : at + hi - lo] = t.astype(BF)
                at += hi - lo

    pending = {}

    def core_send(k):
        pending[k, 0] = [
            send(SB0[k][p].at[1 - c], R0[k][p], rs_s.at[k, 0, p], rs_r.at[k, 0, p], sibling) for p in range(3)
        ]

    def halve(k, step):
        sent = pending.pop((k, step))
        out = []
        for p in range(3):
            sent[p].wait_recv()
            left = [d for d in (0, 1, 2) if d not in ORDERS[p][:step]]
            mine = A0[k][p].at[c] if step == 0 else ACC[step - 1][k][p]
            got = R0[k][p] if step == 0 else RR[step - 1][k][p]
            d = ORDERS[p][step]

            def half(v):
                return tuple(v if q == d else slice(None) for q in left)

            there, here = half(1 - bit[d]), half(bit[d])
            SB[step][k][p][...] = (mine[there] + got[there].astype(F32)).astype(BF)
            out.append(
                send(SB[step][k][p], RR[step][k][p], rs_s.at[k, step + 1, p], rs_r.at[k, step + 1, p], step_peer[d])
            )
            ACC[step][k][p][...] = mine[here] + got[here].astype(F32)
        pending[k, step + 1] = out

    shifts = {}

    def finish(k):
        sent = pending.pop((k, 3))
        for p in range(3):
            sent[p].wait_recv()
            v = ACC[2][k][p][...] + RR[2][k][p][...].astype(F32)
            at = 0
            for which, lo, hi in CHUNKS[k][p]:
                part = v[at : at + hi - lo]
                at += hi - lo
                if which == "point":
                    fin[3, lo:hi] = part
                elif which[1] == 1:
                    fin[which[0]] = part
                else:
                    rate, tap = which
                    side, sign = (0, 1) if tap == 0 else (1, -1)
                    sh[rate, side] = part.astype(BF)
                    for j, dist in enumerate(FAR[which]):
                        shifts[rate, side, j] = send(
                            sh.at[rate, side], rsh.at[rate, side, j], sh_s.at[rate, side, j], sh_r.at[rate, side, j],
                            lon_peer(sign * dist),
                        )

    def weights(l0, l1):
        parts = []
        for (s, e), ref in zip(LANES, (wt0, wt1, wt2)):
            lo, hi = max(l0, s), min(l1, e)
            if lo < hi:
                parts.append(
                    jnp.concatenate(
                        [ref[q, GRAY[v][0], GRAY[v][1], w, :, lo - s : hi - s] for q in (0, 1) for v in range(4) for w in (0, 1)],
                        axis=0,
                    )
                )
        return parts[0] if len(parts) == 1 else jnp.concatenate(parts, axis=1)

    def project(branch, value):
        act = jnp.maximum(value * bns[branch : branch + 1] + bnt[branch : branch + 1], 0.0)
        return dot_nt(act.astype(BF), weights(branch * BR, branch * BR + BR))

    def branch_of(rate):
        sub = lax.broadcasted_iota(jnp.int32, (2, 8, 128), 1)
        col = lax.broadcasted_iota(jnp.int32, (2 * OWN, 8, 128), 1)
        total = fin[rate]
        for side, tap in ((0, 0), (1, 2)):
            tiles = []
            for j in range(len(FAR[rate, tap])):
                shifts[rate, side, j].wait_recv()
                tiles.append(rsh[rate, side, j].astype(F32).reshape(OWN, 2, 8, 128))
            if rate == 1:
                moved = tiles[0].reshape(OWN, 16, 128)
                west, east, w_col, e_col = tiles[1], tiles[2], 7, 0
            else:
                flat = [t.reshape(2 * OWN, 8, 128) for t in tiles]
                moved = pltpu.roll(jnp.where(col >= 4, flat[0], flat[1]), 4, 1).reshape(OWN, 16, 128)
                west, east, w_col, e_col = tiles[0], tiles[1], 3, 4
            rim = jnp.zeros((2, 8, 128), F32)
            for j in range(OWN):
                rim = jnp.where(sub == 2 * j, pltpu.roll(west[j], (2 * j - w_col) % 8, 1), rim)
                rim = jnp.where(sub == 2 * j + 1, pltpu.roll(east[j], (2 * j + 1 - e_col) % 8, 1), rim)
            total = total + jnp.concatenate([moved, rim.reshape(1, 16, 128)], axis=0)
        return project(1 + rate, from_tiles(total))

    WT = (wt0, wt1, wt2)
    wsent = {}

    def wt_step(step):
        for p in range(3):
            if step:
                wsent[step - 1, p].wait_recv()
            else:
                loads[f"wt{p}"].wait()
            done = ORDERS[p][:step]
            idx = tuple(slice(None) if d in done else bit[d] for d in range(3)) + (c,)
            ref = WT[p].at[idx]
            wsent[step, p] = send(ref, ref, wt_s.at[step, p], wt_r.at[step, p], step_peer[ORDERS[p][step]])

    def wt_core():
        for p in range(3):
            wsent[2, p].wait_recv()
            ref = WT[p].at[:, :, :, c]
            wsent[3, p] = send(ref, ref, wt_s.at[3, p], wt_r.at[3, p], sibling)

    isent = {}

    def image_start():
        loads["wpool"].wait()
        sums = jnp.sum(feat[...].astype(F32).reshape(ROWS * COLS, CH), axis=0, keepdims=True)
        hi = sums.astype(BF)
        rest = sums - hi.astype(F32)
        mid = rest.astype(BF)
        low = (rest - mid.astype(F32)).astype(BF)
        row = lax.broadcasted_iota(jnp.int32, (16, CH), 0)
        lhs = jnp.where(
            row == 0,
            hi.astype(F32),
            jnp.where(row == 1, mid.astype(F32), jnp.where(row == 2, low.astype(F32), 0.0)),
        ).astype(BF)
        loads["ps"].wait()
        loads["pt"].wait()
        lane = lax.broadcasted_iota(jnp.int32, (1, BR), 1) - chan * 16
        scale = jnp.zeros((1, BR), F32)
        shift = jnp.zeros((1, BR), F32)
        for i in range(16):
            scale = jnp.where(lane == i, ps[i], scale)
            shift = jnp.where(lane == i, pt[i], shift)
        ic[0, 0] = jnp.sum(dot(lhs, wpool[...]), axis=0, keepdims=True)
        ic[0, 1] = scale
        ic[0, 2] = shift

    def image_send():
        for m in range(1, 16):
            isent[2, m] = send(ic.at[0], ic.at[m], ic_s.at[m], ic_r.at[m], chan_peer(m))

    def image_near():
        for m in range(1, 16):
            isent[2, m].wait_recv()
        total = ic[0]
        for m in range(1, 16):
            total = total + ic[m]
        img[...] = total
        ia[0] = total[0]
        for m in near:
            isent[0, m] = send(ia.at[0], ia.at[m], ia_s.at[m], ia_r.at[m], lon_xor(m))

    def image_wide():
        for m in near:
            isent[0, m].wait_recv()
        total = ia[0]
        for m in near:
            total = total + ia[m]
        ib[0] = total
        if blocks > 1:
            pl.semaphore_wait(known, 1)
            for m in range(1, blocks):
                isent[1, m] = send(ib.at[0], ib.at[m], ib_s.at[m], ib_r.at[m], lon_peer(8 * m))

    def image_end():
        total = ib[0]
        for m in range(1, blocks):
            isent[1, m].wait_recv()
            total = total + ib[m]
        return total / (ROWS * COLS * n_lon)

    def tell_known():
        if blocks > 1:
            pl.semaphore_signal(known, inc=1, device_id=lon_peer(-8), device_id_type=MESH)

    esent = []

    def edge_send():
        loads["skip"].wait()
        xs[...] = jnp.zeros((ROWS * COLS, 2 * CH), BF)
        xs[:, :CH] = x2
        xs[:, CH : CH + SK] = skip[...].astype(F32).reshape(ROWS * COLS, SK).astype(BF)
        pick_r = lax.broadcasted_iota(jnp.int32, (ROWS, ROWS * COLS), 0)
        pick_c = lax.broadcasted_iota(jnp.int32, (ROWS, ROWS * COLS), 1)
        for i, col in enumerate((7, 0)):
            edge[i] = dot((pick_c == pick_r * 8 + col).astype(BF), xs[...]).astype(BF)

    def edge_start():
        for i, k in enumerate((1, -1)):
            esent.append(send(edge.at[i], hedge.at[i], ev_s.at[i], ev_r.at[i], lon_peer(k)))

    def edge_place():
        for e in esent:
            e.wait_recv()
        spread_r = lax.broadcasted_iota(jnp.int32, (ROWS * COLS, ROWS), 0)
        spread_c = lax.broadcasted_iota(jnp.int32, (ROWS * COLS, ROWS), 1)
        placed = sum(dot((spread_r == spread_c * 8 + i).astype(BF), hedge[i, :, :CH]) for i in range(2))
        hpad[RIM * 8 : (RIM + ROWS) * 8] = placed.astype(BF)

    def merge_prepare():
        loads["mw"].wait()
        wide_rows = (BR + SK, BR + SK)
        eye = (
            lax.broadcasted_iota(jnp.int32, wide_rows, 0) == lax.broadcasted_iota(jnp.int32, wide_rows, 1)
        ).astype(BF)
        for t in range(3):
            wrow[t, 48:] = jnp.zeros((80, BR + SK), BF)
            wcat[t] = dot_nt(eye, wrow[t]).astype(BF)
        vskip[...] = rows_shifted([dot(xs[:, CH : CH + SK], wcat[t, BR:]) for t in range(3)])
        spread_r = lax.broadcasted_iota(jnp.int32, (ROWS * COLS, ROWS), 0)
        spread_c = lax.broadcasted_iota(jnp.int32, (ROWS * COLS, ROWS), 1)
        outer = dot((spread_r == spread_c * 8 + 7).astype(BF), hedge[0, :, CH:]) + dot(
            (spread_r == spread_c * 8).astype(BF), hedge[1, :, CH:]
        )
        outer = outer[:, :SK].astype(BF)
        vskip_out[...] = rows_shifted([dot(outer, wcat[t, BR:]) for t in range(3)])

    def rows_shifted(parts):
        zero = jnp.zeros((8, 128), F32)
        n = ROWS * COLS
        up = jnp.concatenate([zero, parts[0][: n - 8]], axis=0)
        down = jnp.concatenate([parts[2][8:], zero], axis=0)
        return parts[1] + up + down

    loads["feat"].wait()
    x2 = feat[...].astype(F32).reshape(ROWS * COLS, CH).astype(BF)
    xpad[: RIM * 8] = jnp.zeros((RIM * 8, CH), BF)
    xpad[(RIM + ROWS) * 8 :] = jnp.zeros((RIM * 8, CH), BF)
    hpad[: RIM * 8] = jnp.zeros((RIM * 8, CH), BF)
    hpad[(RIM + ROWS) * 8 :] = jnp.zeros((RIM * 8, CH), BF)
    xpad[RIM * 8 : (RIM + ROWS) * 8] = x2
    image_start()
    edge_send()
    loads["wd2"].wait()
    loads["wd1"].wait()
    compute(0)
    pl.semaphore_wait(barrier, greeted)
    core_send(0)
    edge_start()
    image_send()
    tell_known()
    loads["wd0"].wait()
    compute(1)
    core_send(1)
    halve(0, 0)
    wt_step(0)
    halve(1, 0)
    loads["wpt"].wait()
    halve(0, 1)
    halve(1, 1)
    edge_place()
    compute(2)
    core_send(2)
    image_near()
    halve(0, 2)
    halve(2, 0)
    halve(1, 2)
    wt_step(1)
    finish(0)
    finish(1)
    halve(2, 1)
    image_wide()
    wt_step(2)
    merge_prepare()
    halve(2, 2)
    wt_core()
    loads["bns"].wait()
    loads["bnt"].wait()
    loads["ms"].wait()
    loads["mt"].wait()
    finish(2)
    for p in range(3):
        wsent[3, p].wait_recv()
    proj[...] = project(0, from_tiles(fin[3]))
    proj[...] += branch_of(2)
    proj[...] += branch_of(1)
    proj[...] += branch_of(0)
    gat[beta] = to_tiles(proj[...]).astype(BF)
    gsent = [send(gat.at[beta], gat.at[beta], ga_s.at[m], ga_r.at[m], chan_peer(m)) for m in range(1, 16)]
    offset = project(4, jnp.broadcast_to(image_end(), (32, BR)))[:8]
    for g in gsent:
        g.wait_recv()

    def on_tiles(v):
        return to_tiles(jnp.broadcast_to(v, (8, BR)))[None]

    pooled = jnp.maximum((gat[...].astype(F32) + on_tiles(offset)) * on_tiles(img[1]) + on_tiles(img[2]), 0.0)
    pf = from_tiles(pooled[:, :OWN].reshape(ROWS, 16, 128)).astype(BF)
    rim = from_tiles(pooled[:, OWN]).astype(BF)
    v = vskip[...] + rows_shifted([dot(pf, wcat[t, :BR]) for t in range(3)])
    cell = lax.broadcasted_iota(jnp.int32, (ROWS * COLS, 128), 0)
    held = lax.broadcasted_iota(jnp.int32, (ROWS * COLS, 128), 1)
    row = cell // 8
    west_at = (row // OWN) * 8 + 2 * (row % OWN)
    take = ((cell % 8 == 7) & (held == west_at)) | ((cell % 8 == 0) & (held == west_at + 1))
    outer = dot(take.astype(BF), rim).astype(BF)
    vo = vskip_out[...] + rows_shifted([dot(outer, wcat[t, :BR]) for t in range(3)])
    v3 = v.reshape(ROWS, 8, 128)
    vo3 = vo.reshape(ROWS, 8, 128)
    col = lax.broadcasted_iota(jnp.int32, (ROWS, 8, 128), 1)
    mid = pltpu.roll(v3, 112, 2)
    left = pltpu.roll(jnp.where(col == 7, vo3, v3), 1, 1)
    right = pltpu.roll(pltpu.roll(jnp.where(col == 0, vo3, v3), 96, 2), 7, 1)
    total = mid + left + right
    lane = lax.broadcasted_iota(jnp.int32, (1, 1, 128), 2)
    scale = jnp.zeros((1, 1, 128), F32)
    shift = jnp.zeros((1, 1, 128), F32)
    for i in range(16):
        scale = jnp.where(lane == i, ms[i], scale)
        shift = jnp.where(lane == i, mt[i], shift)
    out_ref[...] = jnp.maximum(total * scale + shift, 0.0)[:, :, :16].astype(BF)
    for cp in sends:
        cp.wait_send()


def body(features, w_point, w_dilated, w_pool, bn_scale, bn_shift, proj_weight, proj_scale, proj_shift, skip, merge_weight, merge_scale, merge_shift):
    n_lon = lax.axis_size("lon")
    vm = pltpu.VMEM
    dma = pltpu.SemaphoreType.DMA
    t3, t4 = (OWN, 16, 128), (OWN + 1, 16, 128)
    steps = []
    for chunk in TILES:
        for n in chunk:
            for i, rest in enumerate(((2, 2, 2), (2, 2), (2,), ())):
                own = ((2,) + rest if i == 0 else rest) + (n, 16, 128)
                steps += [vm(own, F32), vm(own, BF), vm(rest + (n, 16, 128), BF)]
    scratch = (
        [
            vm((ROWS, COLS, CH), BF), vm((CH, BR), BF), vm((3, 3, 3, CH, BR), BF), vm((CH, BR), BF),
            vm((5, BR), F32), vm((5, BR), F32), pltpu.SMEM((16,), F32), pltpu.SMEM((16,), F32),
            vm((ROWS, COLS, SK), BF), pltpu.SMEM((16,), F32), pltpu.SMEM((16,), F32),
            vm((ROWS * COLS, 2 * CH), BF), vm(((ROWS + 2 * RIM) * 8, CH), BF), vm(((ROWS + 2 * RIM) * 8, CH), BF),
            vm((2, ROWS, 2 * CH), BF), vm((2, ROWS, 2 * CH), BF),
        ]
        + steps
        + [
            vm((4,) + t4, F32), vm((3, 2) + t3, BF), vm((3, 2, 3) + t3, BF),
            vm((2, 2, 2, 2, 16, 512), BF), vm((2, 2, 2, 2, 16, 384), BF), vm((2, 2, 2, 2, 16, 384), BF),
            vm((8, 1, BR), F32), vm((4, 1, BR), F32), vm((16, 3, 1, BR), F32), vm((3, 1, BR), F32),
            vm((16,) + t4, BF), vm((3, 128, BR + SK), BF), vm((3, BR + SK, 128), BF),
            vm((ROWS * COLS, 128), F32), vm((ROWS * COLS, 128), F32), vm((32, BR), F32),
            dma((13,)), dma((3, 5)), dma((3, 3)), pltpu.SemaphoreType.REGULAR,
            dma((3, 4, 3)), dma((3, 4, 3)), dma((3, 2, 3)), dma((3, 2, 3)), dma((4, 3)), dma((4, 3)),
            dma((8,)), dma((8,)), dma((4,)), dma((4,)), dma((16,)), dma((16,)), dma((16,)), dma((16,)), dma((2,)), dma((2,)),
        ]
    )
    return pl.pallas_call(
        functools.partial(kernel, n_lon),
        out_shape=jax.ShapeDtypeStruct((ROWS, COLS, 16), BF),
        in_specs=[pl.BlockSpec(memory_space=pltpu.HBM)] * 13,
        out_specs=pl.BlockSpec(memory_space=pltpu.VMEM),
        scratch_shapes=scratch,
        compiler_params=pltpu.CompilerParams(
            collective_id=0, has_side_effects=True, vmem_limit_bytes=63 * 1024 * 1024
        ),
        name="aspp_head",
    )(features, w_point, w_dilated, w_pool, bn_scale, bn_shift, jnp.swapaxes(proj_weight, 1, 2), proj_scale, proj_shift, skip, jnp.swapaxes(merge_weight, 2, 3), merge_scale, merge_shift)


def solution(mesh):
    return jax.shard_map(
        body,
        mesh=mesh,
        in_specs=(
            P(None, "lon", "chan"),
            P("chan", None),
            P(None, None, None, "chan", None),
            P("chan", None),
            P(),
            P(),
            P(None, None, "chan"),
            P("chan"),
            P("chan"),
            P(None, "lon", None),
            P(None, None, None, "chan"),
            P("chan"),
            P("chan"),
        ),
        out_specs=P(None, "lon", "chan"),
        check_vma=False,
    )
```

```python
import functools

import jax
import jax.numpy as jnp
from jax import lax
from jax.experimental import pallas as pl
from jax.experimental.pallas import tpu as pltpu
from jax.sharding import PartitionSpec as P

BF = jnp.bfloat16
F32 = jnp.float32
MESH = pl.DeviceIdType.MESH

ROWS, COLS, CH, BR, SK = 48, 8, 128, 256, 48
OWN = 3
RIM = 36
DIL = (12, 24, 36)
CHUNKS = (
    ((((2, 0), 0, 3),), (((2, 2), 0, 3),), (((1, 0), 0, 3),)),
    ((((1, 2), 0, 3),), (((0, 0), 0, 3),), (((0, 2), 0, 3),)),
    (
        (((2, 1), 0, 3), ("point", 0, 1)),
        (((1, 1), 0, 3), ("point", 1, 2)),
        (((0, 1), 0, 3), ("point", 2, 3)),
    ),
)
TILES = [[sum(hi - lo for _, lo, hi in part) for part in chunk] for chunk in CHUNKS]
ORDERS = ((0, 2, 1), (2, 1, 0), (1, 0, 2))
LANES = ((0, 512), (512, 896), (896, 1280))
FAR = {(0, 0): (2, 1), (0, 2): (1, 2), (1, 0): (3, 4, 2), (1, 2): (3, 2, 4), (2, 0): (5, 4), (2, 2): (4, 5)}
GRAY = ((0, 0), (0, 1), (1, 1), (1, 0))


def dot(a, b):
    return lax.dot_general(a, b, (((1,), (0,)), ((), ())), preferred_element_type=F32)


def dot_nt(a, b):
    return lax.dot_general(a, b, (((1,), (1,)), ((), ())), preferred_element_type=F32)


def to_tiles(v):
    n = v.shape[0] // 8
    lo = v[:, :128].reshape(n, 8, 128)
    hi = v[:, 128:].reshape(n, 8, 128)
    return jnp.concatenate([lo, hi], axis=1)


def from_tiles(t):
    n = t.shape[0]
    lo = t[:, :8].reshape(n * 8, 128)
    hi = t[:, 8:].reshape(n * 8, 128)
    return jnp.concatenate([lo, hi], axis=1)


class Several:
    def __init__(self):
        self.copies = []

    def wait(self):
        for cp in self.copies:
            cp.wait()


def kernel(
    n_lon,
    feat_h, wpt_h, wd_h, wpool_h, bns_h, bnt_h, pw_h, ps_h, pt_h, skip_h, mw_h, ms_h, mt_h,
    out_ref,
    *refs,
):
    (feat, wpt, wd, wpool, bns, bnt, ps, pt, skip, ms, mt, xs, xpad, hpad, edge, hedge), refs = refs[:16], refs[16:]
    steps, refs = refs[:108], refs[108:]
    (
        fin, sh, rsh, wt0, wt1, wt2, ia, ib, ic, img, gat, wrow, wcat, vskip, vskip_out, proj,
        ld_sem, pw_sem, mw_sem, known,
        rs_s, rs_r, sh_s, sh_r, wt_s, wt_r, ia_s, ia_r, ib_s, ib_r, ic_s, ic_r, ga_s, ga_r, ev_s, ev_r, hb, hbs, hr, hr_s, hr_r,
    ) = refs
    A0, SB0, R0 = ([[steps[(k * 3 + p) * 12 + i] for p in range(3)] for k in range(3)] for i in range(3))
    ACC, SB, RR = (
        [[[steps[(k * 3 + p) * 12 + 3 * (q + 1) + i] for p in range(3)] for k in range(3)] for q in range(3)] for i in range(3)
    )
    lon = lax.axis_index("lon")
    chan = lax.axis_index("chan")
    a = chan // 8
    y = (chan // 2) % 4
    c = chan % 2
    bit = (a, y // 2, (y % 2 + y // 2) % 2)
    beta = c * 8 + bit[0] * 4 + bit[1] * 2 + bit[2]

    loads = {}
    for i, (name, src, dst) in enumerate(
        [
            ("feat", feat_h, feat), ("wd2", wd_h.at[2], wd.at[2]), ("wd1", wd_h.at[1], wd.at[1]),
            ("wd0", wd_h.at[0], wd.at[0]), ("wpt", wpt_h, wpt), ("wpool", wpool_h, wpool),
            ("ps", ps_h, ps), ("pt", pt_h, pt), ("bns", bns_h, bns), ("bnt", bnt_h, bnt), ("skip", skip_h, skip),
            ("ms", ms_h, ms), ("mt", mt_h, mt),
        ]
    ):
        loads[name] = pltpu.make_async_copy(src, dst, ld_sem.at[i])
        loads[name].start()

    for p, ((s, e), ref) in enumerate(zip(LANES, (wt0, wt1, wt2))):
        loads[f"wt{p}"] = Several()
        for b in range(5):
            lo, hi = max(b * BR, s), min(b * BR + BR, e)
            if lo < hi:
                cp = pltpu.make_async_copy(
                    pw_h.at[b, :, lo - b * BR : hi - b * BR],
                    ref.at[bit[0], bit[1], bit[2], c, :, lo - s : hi - s],
                    pw_sem.at[p, b],
                )
                cp.start()
                loads[f"wt{p}"].copies.append(cp)
    loads["mw"] = Several()
    for t in range(3):
        for b in range(3):
            cp = pltpu.make_async_copy(mw_h.at[t, b], wrow.at[t, 16 * b : 16 * b + 16], mw_sem.at[t, b])
            cp.start()
            loads["mw"].copies.append(cp)

    def chan_peer(m):
        mc, mx, mh, ml = (m >> 3) & 1, (m >> 2) & 1, (m >> 1) & 1, m & 1
        pc = 1 - c if mc else c
        pa = 1 - a if mx else a
        flip = y + 1 - 2 * (y % 2)
        py = {(0, 0): y, (0, 1): flip, (1, 0): 3 - y, (1, 1): (y + 2) % 4}[(mh, ml)]
        return (lon, pa * 8 + py * 2 + pc)

    def beta_peer(m):
        bits = [c, *bit]
        masks = [(m >> 3) & 1, (m >> 2) & 1, (m >> 1) & 1, m & 1]
        f = [1 - b if k else b for b, k in zip(bits, masks)]
        return f[0] * 8 + f[1] * 4 + f[2] * 2 + f[3]

    sibling = chan_peer(8)
    step_peer = (chan_peer(4), chan_peer(2), chan_peer(1))

    def lon_peer(k):
        return ((lon + k + n_lon) % n_lon, chan)

    def lon_xor(m):
        out = lon
        for p in range(5):
            if (m >> p) & 1:
                b = (lon // (1 << p)) % 2
                out = out + (1 - 2 * b) * (1 << p)
        return (out, chan)

    near = list(range(1, 8))
    blocks = n_lon // 8

    barrier = pltpu.get_barrier_semaphore()
    greeted = 0
    for dev in (
        [chan_peer(m) for m in range(1, 16)]
        + [lon_peer(k) for k in (1, 2, 3, 4, 5, -1, -2, -3, -4, -5)]
        + [lon_xor(m) for m in near]
        + ([lon_peer(8), lon_peer(-8)] if blocks > 1 else [])
    ):
        pl.semaphore_signal(barrier, inc=1, device_id=dev, device_id_type=MESH)
        greeted += 1

    sends = []

    def send(src, dst, s, r, dev):
        cp = pltpu.make_async_remote_copy(
            src_ref=src, dst_ref=dst, send_sem=s, recv_sem=r, device_id=dev, device_id_type=MESH
        )
        cp.start()
        sends.append(cp)
        return cp

    def taps(ref, d):
        return jnp.concatenate([ref[(RIM + (t - 1) * d) * 8 : (RIM + (t - 1) * d + ROWS) * 8] for t in range(3)], axis=1)

    def field(which, ref):
        if which == "point":
            return to_tiles(dot(ref[RIM * 8 : (RIM + ROWS) * 8], wpt[...])).reshape(16, OWN, 16, 128)
        rate, tap = which
        res = dot(taps(ref, DIL[rate]), wd[rate, :, tap].reshape(3 * CH, BR))
        return to_tiles(res).reshape(16, OWN, 16, 128)

    hsent = []

    def outer_send():
        for f in range(4):
            rim = field("point" if f == 3 else (f, 1), hpad).reshape(16, OWN, 2, 8, 128)
            tile = rim[:, 0] + sum(
                pltpu.roll(rim[:, j].reshape(32, 8, 128), 2 * j, 1).reshape(16, 2, 8, 128) for j in range(1, OWN)
            )
            tile = tile.reshape(16, 16, 128)
            hb[:, f] = tile
            hbs[:, f] = tile.astype(BF)
        for m in range(1, 16):
            hsent.append(send(hbs.at[beta_peer(m)], hr.at[m], hr_s.at[m], hr_r.at[m], chan_peer(m)))

    def outer_end():
        total = hb[beta]
        for m in range(1, 16):
            hsent[m - 1].wait_recv()
            total = total + hr[m].astype(F32)
        for f in range(4):
            fin[f, OWN] = total[f]

    def compute(k):
        made = {}
        for p in range(3):
            at = 0
            for which, lo, hi in CHUNKS[k][p]:
                if which not in made:
                    made[which] = field(which, xpad)
                t = made[which][:, lo:hi].reshape(2, 2, 2, 2, hi - lo, 16, 128)
                A0[k][p][:, :, :, :, at : at + hi - lo] = t
                SB0[k][p][:, :, :, :, at : at + hi - lo] = t.astype(BF)
                at += hi - lo

    pending = {}

    def core_send(k):
        pending[k, 0] = [
            send(SB0[k][p].at[1 - c], R0[k][p], rs_s.at[k, 0, p], rs_r.at[k, 0, p], sibling) for p in range(3)
        ]

    def halve(k, step):
        sent = pending.pop((k, step))
        out = []
        for p in range(3):
            sent[p].wait_recv()
            left = [d for d in (0, 1, 2) if d not in ORDERS[p][:step]]
            mine = A0[k][p].at[c] if step == 0 else ACC[step - 1][k][p]
            got = R0[k][p] if step == 0 else RR[step - 1][k][p]
            d = ORDERS[p][step]

            def half(v):
                return tuple(v if q == d else slice(None) for q in left)

            there, here = half(1 - bit[d]), half(bit[d])
            SB[step][k][p][...] = (mine[there] + got[there].astype(F32)).astype(BF)
            out.append(
                send(SB[step][k][p], RR[step][k][p], rs_s.at[k, step + 1, p], rs_r.at[k, step + 1, p], step_peer[d])
            )
            ACC[step][k][p][...] = mine[here] + got[here].astype(F32)
        pending[k, step + 1] = out

    shifts = {}

    def finish(k):
        sent = pending.pop((k, 3))
        for p in range(3):
            sent[p].wait_recv()
            v = ACC[2][k][p][...] + RR[2][k][p][...].astype(F32)
            at = 0
            for which, lo, hi in CHUNKS[k][p]:
                part = v[at : at + hi - lo]
                at += hi - lo
                if which == "point":
                    fin[3, lo:hi] = part
                elif which[1] == 1:
                    fin[which[0], :OWN] = part
                else:
                    rate, tap = which
                    side, sign = (0, 1) if tap == 0 else (1, -1)
                    sh[rate, side] = part.astype(BF)
                    for j, dist in enumerate(FAR[which]):
                        shifts[rate, side, j] = send(
                            sh.at[rate, side], rsh.at[rate, side, j], sh_s.at[rate, side, j], sh_r.at[rate, side, j],
                            lon_peer(sign * dist),
                        )

    def weights(l0, l1):
        parts = []
        for (s, e), ref in zip(LANES, (wt0, wt1, wt2)):
            lo, hi = max(l0, s), min(l1, e)
            if lo < hi:
                parts.append(
                    jnp.concatenate(
                        [ref[q, GRAY[v][0], GRAY[v][1], w, :, lo - s : hi - s] for q in (0, 1) for v in range(4) for w in (0, 1)],
                        axis=0,
                    )
                )
        return parts[0] if len(parts) == 1 else jnp.concatenate(parts, axis=1)

    def project(branch, value):
        act = jnp.maximum(value * bns[branch : branch + 1] + bnt[branch : branch + 1], 0.0)
        return dot_nt(act.astype(BF), weights(branch * BR, branch * BR + BR))

    def branch_of(rate):
        sub = lax.broadcasted_iota(jnp.int32, (2, 8, 128), 1)
        col = lax.broadcasted_iota(jnp.int32, (2 * OWN, 8, 128), 1)
        total = fin[rate]
        for side, tap in ((0, 0), (1, 2)):
            tiles = []
            for j in range(len(FAR[rate, tap])):
                shifts[rate, side, j].wait_recv()
                tiles.append(rsh[rate, side, j].astype(F32).reshape(OWN, 2, 8, 128))
            if rate == 1:
                moved = tiles[0].reshape(OWN, 16, 128)
                west, east, w_col, e_col = tiles[1], tiles[2], 7, 0
            else:
                flat = [t.reshape(2 * OWN, 8, 128) for t in tiles]
                moved = pltpu.roll(jnp.where(col >= 4, flat[0], flat[1]), 4, 1).reshape(OWN, 16, 128)
                west, east, w_col, e_col = tiles[0], tiles[1], 3, 4
            rim = jnp.zeros((2, 8, 128), F32)
            for j in range(OWN):
                rim = jnp.where(sub == 2 * j, pltpu.roll(west[j], (2 * j - w_col) % 8, 1), rim)
                rim = jnp.where(sub == 2 * j + 1, pltpu.roll(east[j], (2 * j + 1 - e_col) % 8, 1), rim)
            total = total + jnp.concatenate([moved, rim.reshape(1, 16, 128)], axis=0)
        return project(1 + rate, from_tiles(total))

    WT = (wt0, wt1, wt2)
    wsent = {}

    def wt_step(step):
        for p in range(3):
            if step:
                wsent[step - 1, p].wait_recv()
            else:
                loads[f"wt{p}"].wait()
            done = ORDERS[p][:step]
            idx = tuple(slice(None) if d in done else bit[d] for d in range(3)) + (c,)
            ref = WT[p].at[idx]
            wsent[step, p] = send(ref, ref, wt_s.at[step, p], wt_r.at[step, p], step_peer[ORDERS[p][step]])

    def wt_core():
        for p in range(3):
            wsent[2, p].wait_recv()
            ref = WT[p].at[:, :, :, c]
            wsent[3, p] = send(ref, ref, wt_s.at[3, p], wt_r.at[3, p], sibling)

    isent = {}

    def image_start():
        loads["wpool"].wait()
        sums = jnp.sum(feat[...].astype(F32).reshape(ROWS * COLS, CH), axis=0, keepdims=True)
        hi = sums.astype(BF)
        rest = sums - hi.astype(F32)
        mid = rest.astype(BF)
        low = (rest - mid.astype(F32)).astype(BF)
        row = lax.broadcasted_iota(jnp.int32, (16, CH), 0)
        lhs = jnp.where(
            row == 0,
            hi.astype(F32),
            jnp.where(row == 1, mid.astype(F32), jnp.where(row == 2, low.astype(F32), 0.0)),
        ).astype(BF)
        loads["ps"].wait()
        loads["pt"].wait()
        lane = lax.broadcasted_iota(jnp.int32, (1, BR), 1) - chan * 16
        scale = jnp.zeros((1, BR), F32)
        shift = jnp.zeros((1, BR), F32)
        for i in range(16):
            scale = jnp.where(lane == i, ps[i], scale)
            shift = jnp.where(lane == i, pt[i], shift)
        ic[0, 0] = jnp.sum(dot(lhs, wpool[...]), axis=0, keepdims=True)
        ic[0, 1] = scale
        ic[0, 2] = shift

    def image_send():
        for m in range(1, 16):
            isent[2, m] = send(ic.at[0], ic.at[m], ic_s.at[m], ic_r.at[m], chan_peer(m))

    def image_near():
        for m in range(1, 16):
            isent[2, m].wait_recv()
        total = ic[0]
        for m in range(1, 16):
            total = total + ic[m]
        img[...] = total
        ia[0] = total[0]
        for m in near:
            isent[0, m] = send(ia.at[0], ia.at[m], ia_s.at[m], ia_r.at[m], lon_xor(m))

    def image_wide():
        for m in near:
            isent[0, m].wait_recv()
        total = ia[0]
        for m in near:
            total = total + ia[m]
        ib[0] = total
        if blocks > 1:
            pl.semaphore_wait(known, 1)
            for m in range(1, blocks):
                isent[1, m] = send(ib.at[0], ib.at[m], ib_s.at[m], ib_r.at[m], lon_peer(8 * m))

    def image_end():
        total = ib[0]
        for m in range(1, blocks):
            isent[1, m].wait_recv()
            total = total + ib[m]
        return total / (ROWS * COLS * n_lon)

    def tell_known():
        if blocks > 1:
            pl.semaphore_signal(known, inc=1, device_id=lon_peer(-8), device_id_type=MESH)

    esent = []

    def edge_send():
        loads["skip"].wait()
        xs[...] = jnp.zeros((ROWS * COLS, 2 * CH), BF)
        xs[:, :CH] = x2
        xs[:, CH : CH + SK] = skip[...].astype(F32).reshape(ROWS * COLS, SK).astype(BF)
        pick_r = lax.broadcasted_iota(jnp.int32, (ROWS, ROWS * COLS), 0)
        pick_c = lax.broadcasted_iota(jnp.int32, (ROWS, ROWS * COLS), 1)
        for i, col in enumerate((7, 0)):
            edge[i] = dot((pick_c == pick_r * 8 + col).astype(BF), xs[...]).astype(BF)

    def edge_start():
        for i, k in enumerate((1, -1)):
            esent.append(send(edge.at[i], hedge.at[i], ev_s.at[i], ev_r.at[i], lon_peer(k)))

    def edge_place():
        for e in esent:
            e.wait_recv()
        spread_r = lax.broadcasted_iota(jnp.int32, (ROWS * COLS, ROWS), 0)
        spread_c = lax.broadcasted_iota(jnp.int32, (ROWS * COLS, ROWS), 1)
        placed = sum(dot((spread_r == spread_c * 8 + i).astype(BF), hedge[i, :, :CH]) for i in range(2))
        hpad[RIM * 8 : (RIM + ROWS) * 8] = placed.astype(BF)

    def merge_prepare():
        loads["mw"].wait()
        wide_rows = (BR + SK, BR + SK)
        eye = (
            lax.broadcasted_iota(jnp.int32, wide_rows, 0) == lax.broadcasted_iota(jnp.int32, wide_rows, 1)
        ).astype(BF)
        for t in range(3):
            wrow[t, 48:] = jnp.zeros((80, BR + SK), BF)
            wcat[t] = dot_nt(eye, wrow[t]).astype(BF)
        vskip[...] = rows_shifted([dot(xs[:, CH : CH + SK], wcat[t, BR:]) for t in range(3)])
        spread_r = lax.broadcasted_iota(jnp.int32, (ROWS * COLS, ROWS), 0)
        spread_c = lax.broadcasted_iota(jnp.int32, (ROWS * COLS, ROWS), 1)
        outer = dot((spread_r == spread_c * 8 + 7).astype(BF), hedge[0, :, CH:]) + dot(
            (spread_r == spread_c * 8).astype(BF), hedge[1, :, CH:]
        )
        outer = outer[:, :SK].astype(BF)
        vskip_out[...] = rows_shifted([dot(outer, wcat[t, BR:]) for t in range(3)])

    def rows_shifted(parts):
        zero = jnp.zeros((8, 128), F32)
        n = ROWS * COLS
        up = jnp.concatenate([zero, parts[0][: n - 8]], axis=0)
        down = jnp.concatenate([parts[2][8:], zero], axis=0)
        return parts[1] + up + down

    loads["feat"].wait()
    x2 = feat[...].astype(F32).reshape(ROWS * COLS, CH).astype(BF)
    xpad[: RIM * 8] = jnp.zeros((RIM * 8, CH), BF)
    xpad[(RIM + ROWS) * 8 :] = jnp.zeros((RIM * 8, CH), BF)
    hpad[: RIM * 8] = jnp.zeros((RIM * 8, CH), BF)
    hpad[(RIM + ROWS) * 8 :] = jnp.zeros((RIM * 8, CH), BF)
    xpad[RIM * 8 : (RIM + ROWS) * 8] = x2
    image_start()
    edge_send()
    loads["wd2"].wait()
    loads["wd1"].wait()
    compute(0)
    pl.semaphore_wait(barrier, greeted)
    core_send(0)
    edge_start()
    loads["wd0"].wait()
    compute(1)
    core_send(1)
    image_send()
    halve(0, 0)
    loads["wpt"].wait()
    compute(2)
    core_send(2)
    halve(1, 0)
    halve(2, 0)
    wt_step(0)
    tell_known()
    halve(0, 1)
    halve(1, 1)
    halve(2, 1)
    wt_step(1)
    edge_place()
    halve(0, 2)
    halve(1, 2)
    outer_send()
    image_near()
    halve(2, 2)
    wt_step(2)
    finish(0)
    finish(1)
    finish(2)
    merge_prepare()
    wt_core()
    outer_end()
    image_wide()
    loads["bns"].wait()
    loads["bnt"].wait()
    loads["ms"].wait()
    loads["mt"].wait()
    for p in range(3):
        wsent[3, p].wait_recv()
    proj[...] = project(0, from_tiles(fin[3]))
    proj[...] += branch_of(0)
    proj[...] += branch_of(1)
    proj[...] += branch_of(2)
    gat[beta] = to_tiles(proj[...]).astype(BF)
    gsent = [send(gat.at[beta], gat.at[beta], ga_s.at[m], ga_r.at[m], chan_peer(m)) for m in range(1, 16)]
    offset = project(4, jnp.broadcast_to(image_end(), (32, BR)))[:8]
    for g in gsent:
        g.wait_recv()

    def on_tiles(v):
        return to_tiles(jnp.broadcast_to(v, (8, BR)))[None]

    pooled = jnp.maximum((gat[...].astype(F32) + on_tiles(offset)) * on_tiles(img[1]) + on_tiles(img[2]), 0.0)
    pf = from_tiles(pooled[:, :OWN].reshape(ROWS, 16, 128)).astype(BF)
    rim = from_tiles(pooled[:, OWN]).astype(BF)
    v = vskip[...] + rows_shifted([dot(pf, wcat[t, :BR]) for t in range(3)])
    cell = lax.broadcasted_iota(jnp.int32, (ROWS * COLS, 128), 0)
    held = lax.broadcasted_iota(jnp.int32, (ROWS * COLS, 128), 1)
    row = cell // 8
    west_at = (row // OWN) * 8 + 2 * (row % OWN)
    take = ((cell % 8 == 7) & (held == west_at)) | ((cell % 8 == 0) & (held == west_at + 1))
    outer = dot(take.astype(BF), rim).astype(BF)
    vo = vskip_out[...] + rows_shifted([dot(outer, wcat[t, :BR]) for t in range(3)])
    v3 = v.reshape(ROWS, 8, 128)
    vo3 = vo.reshape(ROWS, 8, 128)
    col = lax.broadcasted_iota(jnp.int32, (ROWS, 8, 128), 1)
    mid = pltpu.roll(v3, 112, 2)
    left = pltpu.roll(jnp.where(col == 7, vo3, v3), 1, 1)
    right = pltpu.roll(pltpu.roll(jnp.where(col == 0, vo3, v3), 96, 2), 7, 1)
    total = mid + left + right
    lane = lax.broadcasted_iota(jnp.int32, (1, 1, 128), 2)
    scale = jnp.zeros((1, 1, 128), F32)
    shift = jnp.zeros((1, 1, 128), F32)
    for i in range(16):
        scale = jnp.where(lane == i, ms[i], scale)
        shift = jnp.where(lane == i, mt[i], shift)
    out_ref[...] = jnp.maximum(total * scale + shift, 0.0)[:, :, :16].astype(BF)
    for cp in sends:
        cp.wait_send()


def body(features, w_point, w_dilated, w_pool, bn_scale, bn_shift, proj_weight, proj_scale, proj_shift, skip, merge_weight, merge_scale, merge_shift):
    n_lon = lax.axis_size("lon")
    vm = pltpu.VMEM
    dma = pltpu.SemaphoreType.DMA
    t3, t4 = (OWN, 16, 128), (OWN + 1, 16, 128)
    steps = []
    for chunk in TILES:
        for n in chunk:
            for i, rest in enumerate(((2, 2, 2), (2, 2), (2,), ())):
                own = ((2,) + rest if i == 0 else rest) + (n, 16, 128)
                steps += [vm(own, F32), vm(own, BF), vm(rest + (n, 16, 128), BF)]
    scratch = (
        [
            vm((ROWS, COLS, CH), BF), vm((CH, BR), BF), vm((3, 3, 3, CH, BR), BF), vm((CH, BR), BF),
            vm((5, BR), F32), vm((5, BR), F32), pltpu.SMEM((16,), F32), pltpu.SMEM((16,), F32),
            vm((ROWS, COLS, SK), BF), pltpu.SMEM((16,), F32), pltpu.SMEM((16,), F32),
            vm((ROWS * COLS, 2 * CH), BF), vm(((ROWS + 2 * RIM) * 8, CH), BF), vm(((ROWS + 2 * RIM) * 8, CH), BF),
            vm((2, ROWS, 2 * CH), BF), vm((2, ROWS, 2 * CH), BF),
        ]
        + steps
        + [
            vm((4,) + t4, F32), vm((3, 2) + t3, BF), vm((3, 2, 3) + t3, BF),
            vm((2, 2, 2, 2, 16, 512), BF), vm((2, 2, 2, 2, 16, 384), BF), vm((2, 2, 2, 2, 16, 384), BF),
            vm((8, 1, BR), F32), vm((4, 1, BR), F32), vm((16, 3, 1, BR), F32), vm((3, 1, BR), F32),
            vm((16,) + t4, BF), vm((3, 128, BR + SK), BF), vm((3, BR + SK, 128), BF),
            vm((ROWS * COLS, 128), F32), vm((ROWS * COLS, 128), F32), vm((32, BR), F32),
            dma((13,)), dma((3, 5)), dma((3, 3)), pltpu.SemaphoreType.REGULAR,
            dma((3, 4, 3)), dma((3, 4, 3)), dma((3, 2, 3)), dma((3, 2, 3)), dma((4, 3)), dma((4, 3)),
            dma((8,)), dma((8,)), dma((4,)), dma((4,)), dma((16,)), dma((16,)), dma((16,)), dma((16,)), dma((2,)), dma((2,)),
            vm((16, 4, 16, 128), F32), vm((16, 4, 16, 128), BF), vm((16, 4, 16, 128), BF), dma((16,)), dma((16,)),
        ]
    )
    return pl.pallas_call(
        functools.partial(kernel, n_lon),
        out_shape=jax.ShapeDtypeStruct((ROWS, COLS, 16), BF),
        in_specs=[pl.BlockSpec(memory_space=pltpu.HBM)] * 13,
        out_specs=pl.BlockSpec(memory_space=pltpu.VMEM),
        scratch_shapes=scratch,
        compiler_params=pltpu.CompilerParams(
            collective_id=0, has_side_effects=True, vmem_limit_bytes=63 * 1024 * 1024
        ),
        name="aspp_head",
    )(features, w_point, w_dilated, w_pool, bn_scale, bn_shift, jnp.swapaxes(proj_weight, 1, 2), proj_scale, proj_shift, skip, jnp.swapaxes(merge_weight, 2, 3), merge_scale, merge_shift)


def solution(mesh):
    return jax.shard_map(
        body,
        mesh=mesh,
        in_specs=(
            P(None, "lon", "chan"),
            P("chan", None),
            P(None, None, None, "chan", None),
            P("chan", None),
            P(),
            P(),
            P(None, None, "chan"),
            P("chan"),
            P("chan"),
            P(None, "lon", None),
            P(None, None, None, "chan"),
            P("chan"),
            P("chan"),
        ),
        out_specs=P(None, "lon", "chan"),
        check_vma=False,
    )
```

```python
import functools

import jax
import jax.numpy as jnp
from jax import lax
from jax.experimental import pallas as pl
from jax.experimental.pallas import tpu as pltpu
from jax.sharding import PartitionSpec as P

BF = jnp.bfloat16
F32 = jnp.float32
MESH = pl.DeviceIdType.MESH

ROWS, COLS, CH, BR, SK = 48, 8, 128, 256, 48
OWN = 3
RIM = 36
DIL = (12, 24, 36)
CHUNKS = (
    ((((2, 0), 0, 3),), (((2, 2), 0, 3),), (((1, 0), 0, 3),)),
    ((((1, 2), 0, 3),), (((0, 0), 0, 3),), (((0, 2), 0, 3),)),
    (
        (((2, 1), 0, 3), ("point", 0, 1)),
        (((1, 1), 0, 3), ("point", 1, 2)),
        (((0, 1), 0, 3), ("point", 2, 3)),
    ),
)
TILES = [[sum(hi - lo for _, lo, hi in part) for part in chunk] for chunk in CHUNKS]
ORDERS = ((0, 2, 1), (2, 1, 0), (1, 0, 2))
LANES = ((0, 512), (512, 896), (896, 1280))
FAR = {(0, 0): (2, 1), (0, 2): (1, 2), (1, 0): (3, 4, 2), (1, 2): (3, 2, 4), (2, 0): (5, 4), (2, 2): (4, 5)}
GRAY = ((0, 0), (0, 1), (1, 1), (1, 0))


def dot(a, b):
    return lax.dot_general(a, b, (((1,), (0,)), ((), ())), preferred_element_type=F32)


def dot_nt(a, b):
    return lax.dot_general(a, b, (((1,), (1,)), ((), ())), preferred_element_type=F32)


def to_tiles(v):
    n = v.shape[0] // 8
    lo = v[:, :128].reshape(n, 8, 128)
    hi = v[:, 128:].reshape(n, 8, 128)
    return jnp.concatenate([lo, hi], axis=1)


def from_tiles(t):
    n = t.shape[0]
    lo = t[:, :8].reshape(n * 8, 128)
    hi = t[:, 8:].reshape(n * 8, 128)
    return jnp.concatenate([lo, hi], axis=1)


class Several:
    def __init__(self):
        self.copies = []

    def wait(self):
        for cp in self.copies:
            cp.wait()


def kernel(
    n_lon,
    feat_h, wpt_h, wd_h, wpool_h, bns_h, bnt_h, pw_h, ps_h, pt_h, skip_h, mw_h, ms_h, mt_h,
    out_ref,
    *refs,
):
    (feat, wpt, wd, wpool, bns, bnt, ps, pt, skip, ms, mt, xs, xpad, hpad, edge, hedge), refs = refs[:16], refs[16:]
    steps, refs = refs[:108], refs[108:]
    (
        fin, sh, rsh, wt0, wt1, wt2, ia, ib, ic, img, gat, wrow, wcat, vskip, vskip_out, proj,
        ld_sem, pw_sem, mw_sem, known,
        rs_s, rs_r, sh_s, sh_r, wt_s, wt_r, ia_s, ia_r, ib_s, ib_r, ic_s, ic_r, ga_s, ga_r, ev_s, ev_r, hb, hbs, hc, hq, hqs, hr, hr_s, hr_r,
    ) = refs
    A0, SB0, R0 = ([[steps[(k * 3 + p) * 12 + i] for p in range(3)] for k in range(3)] for i in range(3))
    ACC, SB, RR = (
        [[[steps[(k * 3 + p) * 12 + 3 * (q + 1) + i] for p in range(3)] for k in range(3)] for q in range(3)] for i in range(3)
    )
    lon = lax.axis_index("lon")
    chan = lax.axis_index("chan")
    a = chan // 8
    y = (chan // 2) % 4
    c = chan % 2
    bit = (a, y // 2, (y % 2 + y // 2) % 2)
    beta = c * 8 + bit[0] * 4 + bit[1] * 2 + bit[2]

    loads = {}
    for i, (name, src, dst) in enumerate(
        [
            ("feat", feat_h, feat), ("wd2", wd_h.at[2], wd.at[2]), ("wd1", wd_h.at[1], wd.at[1]),
            ("wd0", wd_h.at[0], wd.at[0]), ("wpt", wpt_h, wpt), ("wpool", wpool_h, wpool),
            ("ps", ps_h, ps), ("pt", pt_h, pt), ("bns", bns_h, bns), ("bnt", bnt_h, bnt), ("skip", skip_h, skip),
            ("ms", ms_h, ms), ("mt", mt_h, mt),
        ]
    ):
        loads[name] = pltpu.make_async_copy(src, dst, ld_sem.at[i])
        loads[name].start()

    for p, ((s, e), ref) in enumerate(zip(LANES, (wt0, wt1, wt2))):
        loads[f"wt{p}"] = Several()
        for b in range(5):
            lo, hi = max(b * BR, s), min(b * BR + BR, e)
            if lo < hi:
                cp = pltpu.make_async_copy(
                    pw_h.at[b, :, lo - b * BR : hi - b * BR],
                    ref.at[bit[0], bit[1], bit[2], c, :, lo - s : hi - s],
                    pw_sem.at[p, b],
                )
                cp.start()
                loads[f"wt{p}"].copies.append(cp)
    loads["mw"] = Several()
    for t in range(3):
        for b in range(3):
            cp = pltpu.make_async_copy(mw_h.at[t, b], wrow.at[t, 16 * b : 16 * b + 16], mw_sem.at[t, b])
            cp.start()
            loads["mw"].copies.append(cp)

    def chan_peer(m):
        mc, mx, mh, ml = (m >> 3) & 1, (m >> 2) & 1, (m >> 1) & 1, m & 1
        pc = 1 - c if mc else c
        pa = 1 - a if mx else a
        flip = y + 1 - 2 * (y % 2)
        py = {(0, 0): y, (0, 1): flip, (1, 0): 3 - y, (1, 1): (y + 2) % 4}[(mh, ml)]
        return (lon, pa * 8 + py * 2 + pc)

    def beta_peer(m):
        bits = [c, *bit]
        masks = [(m >> 3) & 1, (m >> 2) & 1, (m >> 1) & 1, m & 1]
        f = [1 - b if k else b for b, k in zip(bits, masks)]
        return f[0] * 8 + f[1] * 4 + f[2] * 2 + f[3]

    sibling = chan_peer(8)
    step_peer = (chan_peer(4), chan_peer(2), chan_peer(1))

    def lon_peer(k):
        return ((lon + k + n_lon) % n_lon, chan)

    def lon_xor(m):
        out = lon
        for p in range(5):
            if (m >> p) & 1:
                b = (lon // (1 << p)) % 2
                out = out + (1 - 2 * b) * (1 << p)
        return (out, chan)

    near = list(range(1, 8))
    blocks = n_lon // 8

    barrier = pltpu.get_barrier_semaphore()
    greeted = 0
    for dev in (
        [chan_peer(m) for m in range(1, 16)]
        + [lon_peer(k) for k in (1, 2, 3, 4, 5, -1, -2, -3, -4, -5)]
        + [lon_xor(m) for m in near]
        + ([lon_peer(8), lon_peer(-8)] if blocks > 1 else [])
    ):
        pl.semaphore_signal(barrier, inc=1, device_id=dev, device_id_type=MESH)
        greeted += 1

    sends = []

    def send(src, dst, s, r, dev):
        cp = pltpu.make_async_remote_copy(
            src_ref=src, dst_ref=dst, send_sem=s, recv_sem=r, device_id=dev, device_id_type=MESH
        )
        cp.start()
        sends.append(cp)
        return cp

    def taps(ref, d):
        return jnp.concatenate([ref[(RIM + (t - 1) * d) * 8 : (RIM + (t - 1) * d + ROWS) * 8] for t in range(3)], axis=1)

    def field(which, ref):
        if which == "point":
            return to_tiles(dot(ref[RIM * 8 : (RIM + ROWS) * 8], wpt[...])).reshape(16, OWN, 16, 128)
        rate, tap = which
        res = dot(taps(ref, DIL[rate]), wd[rate, :, tap].reshape(3 * CH, BR))
        return to_tiles(res).reshape(16, OWN, 16, 128)

    hsent = []

    def outer_send():
        for f in range(4):
            rim = field("point" if f == 3 else (f, 1), hpad).reshape(16, OWN, 2, 8, 128)
            tile = rim[:, 0] + sum(
                pltpu.roll(rim[:, j].reshape(32, 8, 128), 2 * j, 1).reshape(16, 2, 8, 128) for j in range(1, OWN)
            )
            tile = tile.reshape(16, 16, 128)
            hb[:, f] = tile
            hbs[:, f] = tile.astype(BF)
        hsent.append(send(hbs.at[pl.ds((1 - c) * 8, 8)], hc, hr_s.at[8], hr_r.at[8], sibling))

    def outer_chips():
        hsent[0].wait_recv()
        hq[...] = hb[pl.ds(c * 8, 8)] + hc[...].astype(F32)
        hqs[...] = hq[...].astype(BF)
        for m in range(1, 8):
            hsent.append(send(hqs.at[beta_peer(m) - 8 * c], hr.at[m], hr_s.at[m], hr_r.at[m], chan_peer(m)))

    def outer_end():
        total = hq[beta - 8 * c]
        for m in range(1, 8):
            hsent[m].wait_recv()
            total = total + hr[m].astype(F32)
        for f in range(4):
            fin[f, OWN] = total[f]

    def compute(k):
        made = {}
        for p in range(3):
            at = 0
            for which, lo, hi in CHUNKS[k][p]:
                if which not in made:
                    made[which] = field(which, xpad)
                t = made[which][:, lo:hi].reshape(2, 2, 2, 2, hi - lo, 16, 128)
                A0[k][p][:, :, :, :, at : at + hi - lo] = t
                SB0[k][p][:, :, :, :, at : at + hi - lo] = t.astype(BF)
                at += hi - lo

    pending = {}

    def core_send(k):
        pending[k, 0] = [
            send(SB0[k][p].at[1 - c], R0[k][p], rs_s.at[k, 0, p], rs_r.at[k, 0, p], sibling) for p in range(3)
        ]

    def halve(k, step):
        sent = pending.pop((k, step))
        out = []
        for p in range(3):
            sent[p].wait_recv()
            left = [d for d in (0, 1, 2) if d not in ORDERS[p][:step]]
            mine = A0[k][p].at[c] if step == 0 else ACC[step - 1][k][p]
            got = R0[k][p] if step == 0 else RR[step - 1][k][p]
            d = ORDERS[p][step]

            def half(v):
                return tuple(v if q == d else slice(None) for q in left)

            there, here = half(1 - bit[d]), half(bit[d])
            SB[step][k][p][...] = (mine[there] + got[there].astype(F32)).astype(BF)
            out.append(
                send(SB[step][k][p], RR[step][k][p], rs_s.at[k, step + 1, p], rs_r.at[k, step + 1, p], step_peer[d])
            )
            ACC[step][k][p][...] = mine[here] + got[here].astype(F32)
        pending[k, step + 1] = out

    shifts = {}

    def finish(k):
        sent = pending.pop((k, 3))
        for p in range(3):
            sent[p].wait_recv()
            v = ACC[2][k][p][...] + RR[2][k][p][...].astype(F32)
            at = 0
            for which, lo, hi in CHUNKS[k][p]:
                part = v[at : at + hi - lo]
                at += hi - lo
                if which == "point":
                    fin[3, lo:hi] = part
                elif which[1] == 1:
                    fin[which[0], :OWN] = part
                else:
                    rate, tap = which
                    side, sign = (0, 1) if tap == 0 else (1, -1)
                    sh[rate, side] = part.astype(BF)
                    for j, dist in enumerate(FAR[which]):
                        shifts[rate, side, j] = send(
                            sh.at[rate, side], rsh.at[rate, side, j], sh_s.at[rate, side, j], sh_r.at[rate, side, j],
                            lon_peer(sign * dist),
                        )

    def weights(l0, l1):
        parts = []
        for (s, e), ref in zip(LANES, (wt0, wt1, wt2)):
            lo, hi = max(l0, s), min(l1, e)
            if lo < hi:
                parts.append(
                    jnp.concatenate(
                        [ref[q, GRAY[v][0], GRAY[v][1], w, :, lo - s : hi - s] for q in (0, 1) for v in range(4) for w in (0, 1)],
                        axis=0,
                    )
                )
        return parts[0] if len(parts) == 1 else jnp.concatenate(parts, axis=1)

    def project(branch, value):
        act = jnp.maximum(value * bns[branch : branch + 1] + bnt[branch : branch + 1], 0.0)
        return dot_nt(act.astype(BF), weights(branch * BR, branch * BR + BR))

    def branch_of(rate):
        sub = lax.broadcasted_iota(jnp.int32, (2, 8, 128), 1)
        col = lax.broadcasted_iota(jnp.int32, (2 * OWN, 8, 128), 1)
        total = fin[rate]
        for side, tap in ((0, 0), (1, 2)):
            tiles = []
            for j in range(len(FAR[rate, tap])):
                shifts[rate, side, j].wait_recv()
                tiles.append(rsh[rate, side, j].astype(F32).reshape(OWN, 2, 8, 128))
            if rate == 1:
                moved = tiles[0].reshape(OWN, 16, 128)
                west, east, w_col, e_col = tiles[1], tiles[2], 7, 0
            else:
                flat = [t.reshape(2 * OWN, 8, 128) for t in tiles]
                moved = pltpu.roll(jnp.where(col >= 4, flat[0], flat[1]), 4, 1).reshape(OWN, 16, 128)
                west, east, w_col, e_col = tiles[0], tiles[1], 3, 4
            rim = jnp.zeros((2, 8, 128), F32)
            for j in range(OWN):
                rim = jnp.where(sub == 2 * j, pltpu.roll(west[j], (2 * j - w_col) % 8, 1), rim)
                rim = jnp.where(sub == 2 * j + 1, pltpu.roll(east[j], (2 * j + 1 - e_col) % 8, 1), rim)
            total = total + jnp.concatenate([moved, rim.reshape(1, 16, 128)], axis=0)
        return project(1 + rate, from_tiles(total))

    WT = (wt0, wt1, wt2)
    wsent = {}

    def wt_step(step):
        for p in range(3):
            if step:
                wsent[step - 1, p].wait_recv()
            else:
                loads[f"wt{p}"].wait()
            done = ORDERS[p][:step]
            idx = tuple(slice(None) if d in done else bit[d] for d in range(3)) + (c,)
            ref = WT[p].at[idx]
            wsent[step, p] = send(ref, ref, wt_s.at[step, p], wt_r.at[step, p], step_peer[ORDERS[p][step]])

    def wt_core():
        for p in range(3):
            wsent[2, p].wait_recv()
            ref = WT[p].at[:, :, :, c]
            wsent[3, p] = send(ref, ref, wt_s.at[3, p], wt_r.at[3, p], sibling)

    isent = {}

    def image_start():
        loads["wpool"].wait()
        sums = jnp.sum(feat[...].astype(F32).reshape(ROWS * COLS, CH), axis=0, keepdims=True)
        hi = sums.astype(BF)
        rest = sums - hi.astype(F32)
        mid = rest.astype(BF)
        low = (rest - mid.astype(F32)).astype(BF)
        row = lax.broadcasted_iota(jnp.int32, (16, CH), 0)
        lhs = jnp.where(
            row == 0,
            hi.astype(F32),
            jnp.where(row == 1, mid.astype(F32), jnp.where(row == 2, low.astype(F32), 0.0)),
        ).astype(BF)
        loads["ps"].wait()
        loads["pt"].wait()
        lane = lax.broadcasted_iota(jnp.int32, (1, BR), 1) - chan * 16
        scale = jnp.zeros((1, BR), F32)
        shift = jnp.zeros((1, BR), F32)
        for i in range(16):
            scale = jnp.where(lane == i, ps[i], scale)
            shift = jnp.where(lane == i, pt[i], shift)
        ic[0, 0] = jnp.sum(dot(lhs, wpool[...]), axis=0, keepdims=True)
        ic[0, 1] = scale
        ic[0, 2] = shift

    def image_send():
        for m in range(1, 16):
            isent[2, m] = send(ic.at[0], ic.at[m], ic_s.at[m], ic_r.at[m], chan_peer(m))

    def image_near():
        for m in range(1, 16):
            isent[2, m].wait_recv()
        total = ic[0]
        for m in range(1, 16):
            total = total + ic[m]
        img[...] = total
        ia[0] = total[0]
        for m in near:
            isent[0, m] = send(ia.at[0], ia.at[m], ia_s.at[m], ia_r.at[m], lon_xor(m))

    def image_wide():
        for m in near:
            isent[0, m].wait_recv()
        total = ia[0]
        for m in near:
            total = total + ia[m]
        ib[0] = total
        if blocks > 1:
            pl.semaphore_wait(known, 1)
            for m in range(1, blocks):
                isent[1, m] = send(ib.at[0], ib.at[m], ib_s.at[m], ib_r.at[m], lon_peer(8 * m))

    def image_end():
        total = ib[0]
        for m in range(1, blocks):
            isent[1, m].wait_recv()
            total = total + ib[m]
        return total / (ROWS * COLS * n_lon)

    def tell_known():
        if blocks > 1:
            pl.semaphore_signal(known, inc=1, device_id=lon_peer(-8), device_id_type=MESH)

    esent = []

    def edge_send():
        loads["skip"].wait()
        xs[...] = jnp.zeros((ROWS * COLS, 2 * CH), BF)
        xs[:, :CH] = x2
        xs[:, CH : CH + SK] = skip[...].astype(F32).reshape(ROWS * COLS, SK).astype(BF)
        pick_r = lax.broadcasted_iota(jnp.int32, (ROWS, ROWS * COLS), 0)
        pick_c = lax.broadcasted_iota(jnp.int32, (ROWS, ROWS * COLS), 1)
        for i, col in enumerate((7, 0)):
            edge[i] = dot((pick_c == pick_r * 8 + col).astype(BF), xs[...]).astype(BF)

    def edge_start():
        for i, k in enumerate((1, -1)):
            esent.append(send(edge.at[i], hedge.at[i], ev_s.at[i], ev_r.at[i], lon_peer(k)))

    def edge_place():
        for e in esent:
            e.wait_recv()
        spread_r = lax.broadcasted_iota(jnp.int32, (ROWS * COLS, ROWS), 0)
        spread_c = lax.broadcasted_iota(jnp.int32, (ROWS * COLS, ROWS), 1)
        placed = sum(dot((spread_r == spread_c * 8 + i).astype(BF), hedge[i, :, :CH]) for i in range(2))
        hpad[RIM * 8 : (RIM + ROWS) * 8] = placed.astype(BF)

    def merge_prepare():
        loads["mw"].wait()
        wide_rows = (BR + SK, BR + SK)
        eye = (
            lax.broadcasted_iota(jnp.int32, wide_rows, 0) == lax.broadcasted_iota(jnp.int32, wide_rows, 1)
        ).astype(BF)
        for t in range(3):
            wrow[t, 48:] = jnp.zeros((80, BR + SK), BF)
            wcat[t] = dot_nt(eye, wrow[t]).astype(BF)
        vskip[...] = rows_shifted([dot(xs[:, CH : CH + SK], wcat[t, BR:]) for t in range(3)])
        spread_r = lax.broadcasted_iota(jnp.int32, (ROWS * COLS, ROWS), 0)
        spread_c = lax.broadcasted_iota(jnp.int32, (ROWS * COLS, ROWS), 1)
        outer = dot((spread_r == spread_c * 8 + 7).astype(BF), hedge[0, :, CH:]) + dot(
            (spread_r == spread_c * 8).astype(BF), hedge[1, :, CH:]
        )
        outer = outer[:, :SK].astype(BF)
        vskip_out[...] = rows_shifted([dot(outer, wcat[t, BR:]) for t in range(3)])

    def rows_shifted(parts):
        zero = jnp.zeros((8, 128), F32)
        n = ROWS * COLS
        up = jnp.concatenate([zero, parts[0][: n - 8]], axis=0)
        down = jnp.concatenate([parts[2][8:], zero], axis=0)
        return parts[1] + up + down

    loads["feat"].wait()
    x2 = feat[...].astype(F32).reshape(ROWS * COLS, CH).astype(BF)
    xpad[: RIM * 8] = jnp.zeros((RIM * 8, CH), BF)
    xpad[(RIM + ROWS) * 8 :] = jnp.zeros((RIM * 8, CH), BF)
    hpad[: RIM * 8] = jnp.zeros((RIM * 8, CH), BF)
    hpad[(RIM + ROWS) * 8 :] = jnp.zeros((RIM * 8, CH), BF)
    xpad[RIM * 8 : (RIM + ROWS) * 8] = x2
    image_start()
    edge_send()
    loads["wd2"].wait()
    loads["wd1"].wait()
    compute(0)
    pl.semaphore_wait(barrier, greeted)
    core_send(0)
    edge_start()
    loads["wd0"].wait()
    compute(1)
    core_send(1)
    image_send()
    halve(0, 0)
    loads["wpt"].wait()
    compute(2)
    core_send(2)
    halve(1, 0)
    halve(2, 0)
    tell_known()
    halve(0, 1)
    halve(1, 1)
    wt_step(0)
    halve(2, 1)
    edge_place()
    outer_send()
    halve(0, 2)
    halve(1, 2)
    outer_chips()
    image_near()
    wt_step(1)
    halve(2, 2)
    finish(0)
    finish(1)
    finish(2)
    wt_step(2)
    merge_prepare()
    image_wide()
    wt_core()
    outer_end()
    loads["bns"].wait()
    loads["bnt"].wait()
    loads["ms"].wait()
    loads["mt"].wait()
    for p in range(3):
        wsent[3, p].wait_recv()
    proj[...] = project(0, from_tiles(fin[3]))
    proj[...] += branch_of(0)
    proj[...] += branch_of(1)
    proj[...] += branch_of(2)
    gat[beta] = to_tiles(proj[...]).astype(BF)
    gsent = [send(gat.at[beta], gat.at[beta], ga_s.at[m], ga_r.at[m], chan_peer(m)) for m in range(1, 16)]
    offset = project(4, jnp.broadcast_to(image_end(), (32, BR)))[:8]
    for g in gsent:
        g.wait_recv()

    def on_tiles(v):
        return to_tiles(jnp.broadcast_to(v, (8, BR)))[None]

    pooled = jnp.maximum((gat[...].astype(F32) + on_tiles(offset)) * on_tiles(img[1]) + on_tiles(img[2]), 0.0)
    pf = from_tiles(pooled[:, :OWN].reshape(ROWS, 16, 128)).astype(BF)
    rim = from_tiles(pooled[:, OWN]).astype(BF)
    v = vskip[...] + rows_shifted([dot(pf, wcat[t, :BR]) for t in range(3)])
    cell = lax.broadcasted_iota(jnp.int32, (ROWS * COLS, 128), 0)
    held = lax.broadcasted_iota(jnp.int32, (ROWS * COLS, 128), 1)
    row = cell // 8
    west_at = (row // OWN) * 8 + 2 * (row % OWN)
    take = ((cell % 8 == 7) & (held == west_at)) | ((cell % 8 == 0) & (held == west_at + 1))
    outer = dot(take.astype(BF), rim).astype(BF)
    vo = vskip_out[...] + rows_shifted([dot(outer, wcat[t, :BR]) for t in range(3)])
    v3 = v.reshape(ROWS, 8, 128)
    vo3 = vo.reshape(ROWS, 8, 128)
    col = lax.broadcasted_iota(jnp.int32, (ROWS, 8, 128), 1)
    mid = pltpu.roll(v3, 112, 2)
    left = pltpu.roll(jnp.where(col == 7, vo3, v3), 1, 1)
    right = pltpu.roll(pltpu.roll(jnp.where(col == 0, vo3, v3), 96, 2), 7, 1)
    total = mid + left + right
    lane = lax.broadcasted_iota(jnp.int32, (1, 1, 128), 2)
    scale = jnp.zeros((1, 1, 128), F32)
    shift = jnp.zeros((1, 1, 128), F32)
    for i in range(16):
        scale = jnp.where(lane == i, ms[i], scale)
        shift = jnp.where(lane == i, mt[i], shift)
    out_ref[...] = jnp.maximum(total * scale + shift, 0.0)[:, :, :16].astype(BF)
    for cp in sends:
        cp.wait_send()


def body(features, w_point, w_dilated, w_pool, bn_scale, bn_shift, proj_weight, proj_scale, proj_shift, skip, merge_weight, merge_scale, merge_shift):
    n_lon = lax.axis_size("lon")
    vm = pltpu.VMEM
    dma = pltpu.SemaphoreType.DMA
    t3, t4 = (OWN, 16, 128), (OWN + 1, 16, 128)
    steps = []
    for chunk in TILES:
        for n in chunk:
            for i, rest in enumerate(((2, 2, 2), (2, 2), (2,), ())):
                own = ((2,) + rest if i == 0 else rest) + (n, 16, 128)
                steps += [vm(own, F32), vm(own, BF), vm(rest + (n, 16, 128), BF)]
    scratch = (
        [
            vm((ROWS, COLS, CH), BF), vm((CH, BR), BF), vm((3, 3, 3, CH, BR), BF), vm((CH, BR), BF),
            vm((5, BR), F32), vm((5, BR), F32), pltpu.SMEM((16,), F32), pltpu.SMEM((16,), F32),
            vm((ROWS, COLS, SK), BF), pltpu.SMEM((16,), F32), pltpu.SMEM((16,), F32),
            vm((ROWS * COLS, 2 * CH), BF), vm(((ROWS + 2 * RIM) * 8, CH), BF), vm(((ROWS + 2 * RIM) * 8, CH), BF),
            vm((2, ROWS, 2 * CH), BF), vm((2, ROWS, 2 * CH), BF),
        ]
        + steps
        + [
            vm((4,) + t4, F32), vm((3, 2) + t3, BF), vm((3, 2, 3) + t3, BF),
            vm((2, 2, 2, 2, 16, 512), BF), vm((2, 2, 2, 2, 16, 384), BF), vm((2, 2, 2, 2, 16, 384), BF),
            vm((8, 1, BR), F32), vm((4, 1, BR), F32), vm((16, 3, 1, BR), F32), vm((3, 1, BR), F32),
            vm((16,) + t4, BF), vm((3, 128, BR + SK), BF), vm((3, BR + SK, 128), BF),
            vm((ROWS * COLS, 128), F32), vm((ROWS * COLS, 128), F32), vm((32, BR), F32),
            dma((13,)), dma((3, 5)), dma((3, 3)), pltpu.SemaphoreType.REGULAR,
            dma((3, 4, 3)), dma((3, 4, 3)), dma((3, 2, 3)), dma((3, 2, 3)), dma((4, 3)), dma((4, 3)),
            dma((8,)), dma((8,)), dma((4,)), dma((4,)), dma((16,)), dma((16,)), dma((16,)), dma((16,)), dma((2,)), dma((2,)),
            vm((16, 4, 16, 128), F32), vm((16, 4, 16, 128), BF), vm((8, 4, 16, 128), BF),
            vm((8, 4, 16, 128), F32), vm((8, 4, 16, 128), BF), vm((8, 4, 16, 128), BF), dma((9,)), dma((9,)),
        ]
    )
    return pl.pallas_call(
        functools.partial(kernel, n_lon),
        out_shape=jax.ShapeDtypeStruct((ROWS, COLS, 16), BF),
        in_specs=[pl.BlockSpec(memory_space=pltpu.HBM)] * 13,
        out_specs=pl.BlockSpec(memory_space=pltpu.VMEM),
        scratch_shapes=scratch,
        compiler_params=pltpu.CompilerParams(
            collective_id=0, has_side_effects=True, vmem_limit_bytes=63 * 1024 * 1024
        ),
        name="aspp_head",
    )(features, w_point, w_dilated, w_pool, bn_scale, bn_shift, jnp.swapaxes(proj_weight, 1, 2), proj_scale, proj_shift, skip, jnp.swapaxes(merge_weight, 2, 3), merge_scale, merge_shift)


def solution(mesh):
    return jax.shard_map(
        body,
        mesh=mesh,
        in_specs=(
            P(None, "lon", "chan"),
            P("chan", None),
            P(None, None, None, "chan", None),
            P("chan", None),
            P(),
            P(),
            P(None, None, "chan"),
            P("chan"),
            P("chan"),
            P(None, "lon", None),
            P(None, None, None, "chan"),
            P("chan"),
            P("chan"),
        ),
        out_specs=P(None, "lon", "chan"),
        check_vma=False,
    )
```

```python
import functools

import jax
import jax.numpy as jnp
from jax import lax
from jax.experimental import pallas as pl
from jax.experimental.pallas import tpu as pltpu
from jax.sharding import PartitionSpec as P

BF = jnp.bfloat16
F32 = jnp.float32
MESH = pl.DeviceIdType.MESH

ROWS, COLS, CH, BR, SK = 48, 8, 128, 256, 48
OWN = 3
RIM = 36
DIL = (12, 24, 36)
CHUNKS = (
    ((((2, 0), 0, 3),), (((2, 2), 0, 3),), (((1, 0), 0, 3),)),
    ((((1, 2), 0, 3),), (((0, 0), 0, 3),), (((0, 2), 0, 3),)),
    (
        (((2, 1), 0, 3), ("point", 0, 1)),
        (((1, 1), 0, 3), ("point", 1, 2)),
        (((0, 1), 0, 3), ("point", 2, 3)),
    ),
)
TILES = [[sum(hi - lo for _, lo, hi in part) for part in chunk] for chunk in CHUNKS]
ORDERS = ((0, 2, 1), (2, 1, 0), (1, 0, 2))
LANES = ((0, 512), (512, 896), (896, 1280))
FAR = {(0, 0): (2, 1), (0, 2): (1, 2), (1, 0): (3, 4, 2), (1, 2): (3, 2, 4), (2, 0): (5, 4), (2, 2): (4, 5)}
GRAY = ((0, 0), (0, 1), (1, 1), (1, 0))


def dot(a, b):
    return lax.dot_general(a, b, (((1,), (0,)), ((), ())), preferred_element_type=F32)


def dot_nt(a, b):
    return lax.dot_general(a, b, (((1,), (1,)), ((), ())), preferred_element_type=F32)


def to_tiles(v):
    n = v.shape[0] // 8
    lo = v[:, :128].reshape(n, 8, 128)
    hi = v[:, 128:].reshape(n, 8, 128)
    return jnp.concatenate([lo, hi], axis=1)


def from_tiles(t):
    n = t.shape[0]
    lo = t[:, :8].reshape(n * 8, 128)
    hi = t[:, 8:].reshape(n * 8, 128)
    return jnp.concatenate([lo, hi], axis=1)


class Several:
    def __init__(self):
        self.copies = []

    def wait(self):
        for cp in self.copies:
            cp.wait()


def kernel(
    n_lon,
    feat_h, wpt_h, wd_h, wpool_h, bns_h, bnt_h, pw_h, ps_h, pt_h, skip_h, mw_h, ms_h, mt_h,
    out_ref,
    *refs,
):
    (feat, wpt, wd, wpool, bns, bnt, ps, pt, skip, ms, mt, xs, xpad, hpad, edge, hedge), refs = refs[:16], refs[16:]
    steps, refs = refs[:108], refs[108:]
    (
        fin, sh, rsh, wt0, wt1, wt2, ia, ib, ic, img, gat, wrow, wcat, vskip, vskip_out, proj,
        ld_sem, pw_sem, mw_sem, known,
        rs_s, rs_r, sh_s, sh_r, wt_s, wt_r, ia_s, ia_r, ib_s, ib_r, ic_s, ic_r, ga_s, ga_r, ev_s, ev_r, hb, hbs, hc, hq, hqs, hr, hr_s, hr_r,
    ) = refs
    A0, SB0, R0 = ([[steps[(k * 3 + p) * 12 + i] for p in range(3)] for k in range(3)] for i in range(3))
    ACC, SB, RR = (
        [[[steps[(k * 3 + p) * 12 + 3 * (q + 1) + i] for p in range(3)] for k in range(3)] for q in range(3)] for i in range(3)
    )
    lon = lax.axis_index("lon")
    chan = lax.axis_index("chan")
    a = chan // 8
    y = (chan // 2) % 4
    c = chan % 2
    bit = (a, y // 2, (y % 2 + y // 2) % 2)
    beta = c * 8 + bit[0] * 4 + bit[1] * 2 + bit[2]

    loads = {}
    for i, (name, src, dst) in enumerate(
        [
            ("feat", feat_h, feat), ("wd2", wd_h.at[2], wd.at[2]), ("wd1", wd_h.at[1], wd.at[1]),
            ("wd0", wd_h.at[0], wd.at[0]), ("wpt", wpt_h, wpt), ("wpool", wpool_h, wpool),
            ("ps", ps_h, ps), ("pt", pt_h, pt), ("bns", bns_h, bns), ("bnt", bnt_h, bnt), ("skip", skip_h, skip),
            ("ms", ms_h, ms), ("mt", mt_h, mt),
        ]
    ):
        loads[name] = pltpu.make_async_copy(src, dst, ld_sem.at[i])
        loads[name].start()

    for p, ((s, e), ref) in enumerate(zip(LANES, (wt0, wt1, wt2))):
        loads[f"wt{p}"] = Several()
        for b in range(5):
            lo, hi = max(b * BR, s), min(b * BR + BR, e)
            if lo < hi:
                cp = pltpu.make_async_copy(
                    pw_h.at[b, :, lo - b * BR : hi - b * BR],
                    ref.at[bit[0], bit[1], bit[2], c, :, lo - s : hi - s],
                    pw_sem.at[p, b],
                )
                cp.start()
                loads[f"wt{p}"].copies.append(cp)
    loads["mw"] = Several()
    for t in range(3):
        for b in range(3):
            cp = pltpu.make_async_copy(mw_h.at[t, b], wrow.at[t, 16 * b : 16 * b + 16], mw_sem.at[t, b])
            cp.start()
            loads["mw"].copies.append(cp)

    def chan_peer(m):
        mc, mx, mh, ml = (m >> 3) & 1, (m >> 2) & 1, (m >> 1) & 1, m & 1
        pc = 1 - c if mc else c
        pa = 1 - a if mx else a
        flip = y + 1 - 2 * (y % 2)
        py = {(0, 0): y, (0, 1): flip, (1, 0): 3 - y, (1, 1): (y + 2) % 4}[(mh, ml)]
        return (lon, pa * 8 + py * 2 + pc)

    def beta_peer(m):
        bits = [c, *bit]
        masks = [(m >> 3) & 1, (m >> 2) & 1, (m >> 1) & 1, m & 1]
        f = [1 - b if k else b for b, k in zip(bits, masks)]
        return f[0] * 8 + f[1] * 4 + f[2] * 2 + f[3]

    sibling = chan_peer(8)
    step_peer = (chan_peer(4), chan_peer(2), chan_peer(1))

    def lon_peer(k):
        return ((lon + k + n_lon) % n_lon, chan)

    def lon_xor(m):
        out = lon
        for p in range(5):
            if (m >> p) & 1:
                b = (lon // (1 << p)) % 2
                out = out + (1 - 2 * b) * (1 << p)
        return (out, chan)

    near = list(range(1, 8))
    blocks = n_lon // 8

    barrier = pltpu.get_barrier_semaphore()
    greeted = 0
    for dev in (
        [chan_peer(m) for m in range(1, 16)]
        + [lon_peer(k) for k in (1, 2, 3, 4, 5, -1, -2, -3, -4, -5)]
        + [lon_xor(m) for m in near]
        + ([lon_peer(8), lon_peer(-8)] if blocks > 1 else [])
    ):
        pl.semaphore_signal(barrier, inc=1, device_id=dev, device_id_type=MESH)
        greeted += 1

    sends = []

    def send(src, dst, s, r, dev):
        cp = pltpu.make_async_remote_copy(
            src_ref=src, dst_ref=dst, send_sem=s, recv_sem=r, device_id=dev, device_id_type=MESH
        )
        cp.start()
        sends.append(cp)
        return cp

    def taps(ref, d):
        return jnp.concatenate([ref[(RIM + (t - 1) * d) * 8 : (RIM + (t - 1) * d + ROWS) * 8] for t in range(3)], axis=1)

    def field(which, ref):
        if which == "point":
            return to_tiles(dot(ref[RIM * 8 : (RIM + ROWS) * 8], wpt[...])).reshape(16, OWN, 16, 128)
        rate, tap = which
        res = dot(taps(ref, DIL[rate]), wd[rate, :, tap].reshape(3 * CH, BR))
        return to_tiles(res).reshape(16, OWN, 16, 128)

    hsent = []

    def outer_send():
        for f in range(4):
            rim = field("point" if f == 3 else (f, 1), hpad).reshape(16, OWN, 2, 8, 128)
            tile = rim[:, 0] + sum(
                pltpu.roll(rim[:, j].reshape(32, 8, 128), 2 * j, 1).reshape(16, 2, 8, 128) for j in range(1, OWN)
            )
            tile = tile.reshape(16, 16, 128)
            hb[:, f] = tile
            hbs[:, f] = tile.astype(BF)
        hsent.append(send(hbs.at[pl.ds((1 - c) * 8, 8)], hc, hr_s.at[8], hr_r.at[8], sibling))

    def outer_chips():
        hsent[0].wait_recv()
        hq[...] = hb[pl.ds(c * 8, 8)] + hc[...].astype(F32)
        hqs[...] = hq[...].astype(BF)
        for m in range(1, 8):
            hsent.append(send(hqs.at[beta_peer(m) - 8 * c], hr.at[m], hr_s.at[m], hr_r.at[m], chan_peer(m)))

    def outer_end():
        total = hq[beta - 8 * c]
        for m in range(1, 8):
            hsent[m].wait_recv()
            total = total + hr[m].astype(F32)
        for f in range(4):
            fin[f, OWN] = total[f]

    def compute(k):
        made = {}
        for p in range(3):
            at = 0
            for which, lo, hi in CHUNKS[k][p]:
                if which not in made:
                    made[which] = field(which, xpad)
                t = made[which][:, lo:hi].reshape(2, 2, 2, 2, hi - lo, 16, 128)
                A0[k][p][:, :, :, :, at : at + hi - lo] = t
                SB0[k][p][:, :, :, :, at : at + hi - lo] = t.astype(BF)
                at += hi - lo

    pending = {}

    def core_send(k):
        pending[k, 0] = [
            send(SB0[k][p].at[1 - c], R0[k][p], rs_s.at[k, 0, p], rs_r.at[k, 0, p], sibling) for p in range(3)
        ]

    def halve(k, step):
        sent = pending.pop((k, step))
        out = []
        for p in range(3):
            sent[p].wait_recv()
            left = [d for d in (0, 1, 2) if d not in ORDERS[p][:step]]
            mine = A0[k][p].at[c] if step == 0 else ACC[step - 1][k][p]
            got = R0[k][p] if step == 0 else RR[step - 1][k][p]
            d = ORDERS[p][step]

            def half(v):
                return tuple(v if q == d else slice(None) for q in left)

            there, here = half(1 - bit[d]), half(bit[d])
            SB[step][k][p][...] = (mine[there] + got[there].astype(F32)).astype(BF)
            out.append(
                send(SB[step][k][p], RR[step][k][p], rs_s.at[k, step + 1, p], rs_r.at[k, step + 1, p], step_peer[d])
            )
            ACC[step][k][p][...] = mine[here] + got[here].astype(F32)
        pending[k, step + 1] = out

    shifts = {}

    def finish(k):
        sent = pending.pop((k, 3))
        for p in range(3):
            sent[p].wait_recv()
            v = ACC[2][k][p][...] + RR[2][k][p][...].astype(F32)
            at = 0
            for which, lo, hi in CHUNKS[k][p]:
                part = v[at : at + hi - lo]
                at += hi - lo
                if which == "point":
                    fin[3, lo:hi] = part
                elif which[1] == 1:
                    fin[which[0], :OWN] = part
                else:
                    rate, tap = which
                    side, sign = (0, 1) if tap == 0 else (1, -1)
                    sh[rate, side] = part.astype(BF)
                    for j, dist in enumerate(FAR[which]):
                        shifts[rate, side, j] = send(
                            sh.at[rate, side], rsh.at[rate, side, j], sh_s.at[rate, side, j], sh_r.at[rate, side, j],
                            lon_peer(sign * dist),
                        )

    def weights(l0, l1):
        parts = []
        for (s, e), ref in zip(LANES, (wt0, wt1, wt2)):
            lo, hi = max(l0, s), min(l1, e)
            if lo < hi:
                parts.append(
                    jnp.concatenate(
                        [ref[q, GRAY[v][0], GRAY[v][1], w, :, lo - s : hi - s] for q in (0, 1) for v in range(4) for w in (0, 1)],
                        axis=0,
                    )
                )
        return parts[0] if len(parts) == 1 else jnp.concatenate(parts, axis=1)

    def project(branch, value):
        act = jnp.maximum(value * bns[branch : branch + 1] + bnt[branch : branch + 1], 0.0)
        return dot_nt(act.astype(BF), weights(branch * BR, branch * BR + BR))

    def branch_of(rate):
        sub = lax.broadcasted_iota(jnp.int32, (2, 8, 128), 1)
        col = lax.broadcasted_iota(jnp.int32, (2 * OWN, 8, 128), 1)
        total = fin[rate]
        for side, tap in ((0, 0), (1, 2)):
            tiles = []
            for j in range(len(FAR[rate, tap])):
                shifts[rate, side, j].wait_recv()
                tiles.append(rsh[rate, side, j].astype(F32).reshape(OWN, 2, 8, 128))
            if rate == 1:
                moved = tiles[0].reshape(OWN, 16, 128)
                west, east, w_col, e_col = tiles[1], tiles[2], 7, 0
            else:
                flat = [t.reshape(2 * OWN, 8, 128) for t in tiles]
                moved = pltpu.roll(jnp.where(col >= 4, flat[0], flat[1]), 4, 1).reshape(OWN, 16, 128)
                west, east, w_col, e_col = tiles[0], tiles[1], 3, 4
            rim = jnp.zeros((2, 8, 128), F32)
            for j in range(OWN):
                rim = jnp.where(sub == 2 * j, pltpu.roll(west[j], (2 * j - w_col) % 8, 1), rim)
                rim = jnp.where(sub == 2 * j + 1, pltpu.roll(east[j], (2 * j + 1 - e_col) % 8, 1), rim)
            total = total + jnp.concatenate([moved, rim.reshape(1, 16, 128)], axis=0)
        return project(1 + rate, from_tiles(total))

    WT = (wt0, wt1, wt2)
    wsent = {}

    def wt_step(step):
        for p in range(3):
            if step:
                wsent[step - 1, p].wait_recv()
            else:
                loads[f"wt{p}"].wait()
            done = ORDERS[p][:step]
            idx = tuple(slice(None) if d in done else bit[d] for d in range(3)) + (c,)
            ref = WT[p].at[idx]
            wsent[step, p] = send(ref, ref, wt_s.at[step, p], wt_r.at[step, p], step_peer[ORDERS[p][step]])

    def wt_core():
        for p in range(3):
            wsent[2, p].wait_recv()
            ref = WT[p].at[:, :, :, c]
            wsent[3, p] = send(ref, ref, wt_s.at[3, p], wt_r.at[3, p], sibling)

    isent = {}

    def image_start():
        loads["wpool"].wait()
        sums = jnp.sum(feat[...].astype(F32).reshape(ROWS * COLS, CH), axis=0, keepdims=True)
        hi = sums.astype(BF)
        rest = sums - hi.astype(F32)
        mid = rest.astype(BF)
        low = (rest - mid.astype(F32)).astype(BF)
        row = lax.broadcasted_iota(jnp.int32, (16, CH), 0)
        lhs = jnp.where(
            row == 0,
            hi.astype(F32),
            jnp.where(row == 1, mid.astype(F32), jnp.where(row == 2, low.astype(F32), 0.0)),
        ).astype(BF)
        loads["ps"].wait()
        loads["pt"].wait()
        lane = lax.broadcasted_iota(jnp.int32, (1, BR), 1) - chan * 16
        scale = jnp.zeros((1, BR), F32)
        shift = jnp.zeros((1, BR), F32)
        for i in range(16):
            scale = jnp.where(lane == i, ps[i], scale)
            shift = jnp.where(lane == i, pt[i], shift)
        ic[0, 0] = jnp.sum(dot(lhs, wpool[...]), axis=0, keepdims=True)
        ic[0, 1] = scale
        ic[0, 2] = shift

    def image_send():
        for m in range(1, 16):
            isent[2, m] = send(ic.at[0], ic.at[m], ic_s.at[m], ic_r.at[m], chan_peer(m))

    def image_near():
        for m in range(1, 16):
            isent[2, m].wait_recv()
        total = ic[0]
        for m in range(1, 16):
            total = total + ic[m]
        img[...] = total
        ia[0] = total[0]
        for m in near:
            isent[0, m] = send(ia.at[0], ia.at[m], ia_s.at[m], ia_r.at[m], lon_xor(m))

    def image_wide():
        for m in near:
            isent[0, m].wait_recv()
        total = ia[0]
        for m in near:
            total = total + ia[m]
        ib[0] = total
        if blocks > 1:
            pl.semaphore_wait(known, 1)
            for m in range(1, blocks):
                isent[1, m] = send(ib.at[0], ib.at[m], ib_s.at[m], ib_r.at[m], lon_peer(8 * m))

    def image_end():
        total = ib[0]
        for m in range(1, blocks):
            isent[1, m].wait_recv()
            total = total + ib[m]
        return total / (ROWS * COLS * n_lon)

    def tell_known():
        if blocks > 1:
            pl.semaphore_signal(known, inc=1, device_id=lon_peer(-8), device_id_type=MESH)

    esent = []

    def edge_send():
        loads["skip"].wait()
        xs[...] = jnp.zeros((ROWS * COLS, 2 * CH), BF)
        xs[:, :CH] = x2
        xs[:, CH : CH + SK] = skip[...].astype(F32).reshape(ROWS * COLS, SK).astype(BF)
        pick_r = lax.broadcasted_iota(jnp.int32, (ROWS, ROWS * COLS), 0)
        pick_c = lax.broadcasted_iota(jnp.int32, (ROWS, ROWS * COLS), 1)
        for i, col in enumerate((7, 0)):
            edge[i] = dot((pick_c == pick_r * 8 + col).astype(BF), xs[...]).astype(BF)

    def edge_start():
        for i, k in enumerate((1, -1)):
            esent.append(send(edge.at[i], hedge.at[i], ev_s.at[i], ev_r.at[i], lon_peer(k)))

    def edge_place():
        for e in esent:
            e.wait_recv()
        spread_r = lax.broadcasted_iota(jnp.int32, (ROWS * COLS, ROWS), 0)
        spread_c = lax.broadcasted_iota(jnp.int32, (ROWS * COLS, ROWS), 1)
        placed = sum(dot((spread_r == spread_c * 8 + i).astype(BF), hedge[i, :, :CH]) for i in range(2))
        hpad[RIM * 8 : (RIM + ROWS) * 8] = placed.astype(BF)

    def merge_prepare():
        loads["mw"].wait()
        wide_rows = (BR + SK, BR + SK)
        eye = (
            lax.broadcasted_iota(jnp.int32, wide_rows, 0) == lax.broadcasted_iota(jnp.int32, wide_rows, 1)
        ).astype(BF)
        for t in range(3):
            wrow[t, 48:] = jnp.zeros((80, BR + SK), BF)
            wcat[t] = dot_nt(eye, wrow[t]).astype(BF)
        vskip[...] = rows_shifted([dot(xs[:, CH : CH + SK], wcat[t, BR:]) for t in range(3)])
        spread_r = lax.broadcasted_iota(jnp.int32, (ROWS * COLS, ROWS), 0)
        spread_c = lax.broadcasted_iota(jnp.int32, (ROWS * COLS, ROWS), 1)
        outer = dot((spread_r == spread_c * 8 + 7).astype(BF), hedge[0, :, CH:]) + dot(
            (spread_r == spread_c * 8).astype(BF), hedge[1, :, CH:]
        )
        outer = outer[:, :SK].astype(BF)
        vskip_out[...] = rows_shifted([dot(outer, wcat[t, BR:]) for t in range(3)])

    def rows_shifted(parts):
        zero = jnp.zeros((8, 128), F32)
        n = ROWS * COLS
        up = jnp.concatenate([zero, parts[0][: n - 8]], axis=0)
        down = jnp.concatenate([parts[2][8:], zero], axis=0)
        return parts[1] + up + down

    loads["feat"].wait()
    x2 = feat[...].astype(F32).reshape(ROWS * COLS, CH).astype(BF)
    xpad[: RIM * 8] = jnp.zeros((RIM * 8, CH), BF)
    xpad[(RIM + ROWS) * 8 :] = jnp.zeros((RIM * 8, CH), BF)
    hpad[: RIM * 8] = jnp.zeros((RIM * 8, CH), BF)
    hpad[(RIM + ROWS) * 8 :] = jnp.zeros((RIM * 8, CH), BF)
    xpad[RIM * 8 : (RIM + ROWS) * 8] = x2
    image_start()
    edge_send()
    loads["wd2"].wait()
    loads["wd1"].wait()
    compute(0)
    pl.semaphore_wait(barrier, greeted)
    core_send(0)
    edge_start()
    loads["wd0"].wait()
    compute(1)
    core_send(1)
    image_send()
    halve(0, 0)
    loads["wpt"].wait()
    compute(2)
    core_send(2)
    halve(1, 0)
    halve(2, 0)
    wt_step(0)
    tell_known()
    halve(0, 1)
    halve(1, 1)
    halve(2, 1)
    wt_step(1)
    edge_place()
    outer_send()
    halve(0, 2)
    halve(1, 2)
    outer_chips()
    image_near()
    halve(2, 2)
    wt_step(2)
    finish(0)
    finish(1)
    finish(2)
    merge_prepare()
    wt_core()
    outer_end()
    image_wide()
    loads["bns"].wait()
    loads["bnt"].wait()
    loads["ms"].wait()
    loads["mt"].wait()
    for p in range(3):
        wsent[3, p].wait_recv()
    proj[...] = project(0, from_tiles(fin[3]))
    proj[...] += branch_of(0)
    proj[...] += branch_of(1)
    proj[...] += branch_of(2)
    gat[beta] = to_tiles(proj[...]).astype(BF)
    gsent = [send(gat.at[beta], gat.at[beta], ga_s.at[m], ga_r.at[m], chan_peer(m)) for m in range(1, 16)]
    offset = project(4, jnp.broadcast_to(image_end(), (32, BR)))[:8]
    for g in gsent:
        g.wait_recv()

    def on_tiles(v):
        return to_tiles(jnp.broadcast_to(v, (8, BR)))[None]

    pooled = jnp.maximum((gat[...].astype(F32) + on_tiles(offset)) * on_tiles(img[1]) + on_tiles(img[2]), 0.0)
    pf = from_tiles(pooled[:, :OWN].reshape(ROWS, 16, 128)).astype(BF)
    rim = from_tiles(pooled[:, OWN]).astype(BF)
    v = vskip[...] + rows_shifted([dot(pf, wcat[t, :BR]) for t in range(3)])
    cell = lax.broadcasted_iota(jnp.int32, (ROWS * COLS, 128), 0)
    held = lax.broadcasted_iota(jnp.int32, (ROWS * COLS, 128), 1)
    row = cell // 8
    west_at = (row // OWN) * 8 + 2 * (row % OWN)
    take = ((cell % 8 == 7) & (held == west_at)) | ((cell % 8 == 0) & (held == west_at + 1))
    outer = dot(take.astype(BF), rim).astype(BF)
    vo = vskip_out[...] + rows_shifted([dot(outer, wcat[t, :BR]) for t in range(3)])
    v3 = v.reshape(ROWS, 8, 128)
    vo3 = vo.reshape(ROWS, 8, 128)
    col = lax.broadcasted_iota(jnp.int32, (ROWS, 8, 128), 1)
    mid = pltpu.roll(v3, 112, 2)
    left = pltpu.roll(jnp.where(col == 7, vo3, v3), 1, 1)
    right = pltpu.roll(pltpu.roll(jnp.where(col == 0, vo3, v3), 96, 2), 7, 1)
    total = mid + left + right
    lane = lax.broadcasted_iota(jnp.int32, (1, 1, 128), 2)
    scale = jnp.zeros((1, 1, 128), F32)
    shift = jnp.zeros((1, 1, 128), F32)
    for i in range(16):
        scale = jnp.where(lane == i, ms[i], scale)
        shift = jnp.where(lane == i, mt[i], shift)
    out_ref[...] = jnp.maximum(total * scale + shift, 0.0)[:, :, :16].astype(BF)
    for cp in sends:
        cp.wait_send()


def body(features, w_point, w_dilated, w_pool, bn_scale, bn_shift, proj_weight, proj_scale, proj_shift, skip, merge_weight, merge_scale, merge_shift):
    n_lon = lax.axis_size("lon")
    vm = pltpu.VMEM
    dma = pltpu.SemaphoreType.DMA
    t3, t4 = (OWN, 16, 128), (OWN + 1, 16, 128)
    steps = []
    for chunk in TILES:
        for n in chunk:
            for i, rest in enumerate(((2, 2, 2), (2, 2), (2,), ())):
                own = ((2,) + rest if i == 0 else rest) + (n, 16, 128)
                steps += [vm(own, F32), vm(own, BF), vm(rest + (n, 16, 128), BF)]
    scratch = (
        [
            vm((ROWS, COLS, CH), BF), vm((CH, BR), BF), vm((3, 3, 3, CH, BR), BF), vm((CH, BR), BF),
            vm((5, BR), F32), vm((5, BR), F32), pltpu.SMEM((16,), F32), pltpu.SMEM((16,), F32),
            vm((ROWS, COLS, SK), BF), pltpu.SMEM((16,), F32), pltpu.SMEM((16,), F32),
            vm((ROWS * COLS, 2 * CH), BF), vm(((ROWS + 2 * RIM) * 8, CH), BF), vm(((ROWS + 2 * RIM) * 8, CH), BF),
            vm((2, ROWS, 2 * CH), BF), vm((2, ROWS, 2 * CH), BF),
        ]
        + steps
        + [
            vm((4,) + t4, F32), vm((3, 2) + t3, BF), vm((3, 2, 3) + t3, BF),
            vm((2, 2, 2, 2, 16, 512), BF), vm((2, 2, 2, 2, 16, 384), BF), vm((2, 2, 2, 2, 16, 384), BF),
            vm((8, 1, BR), F32), vm((4, 1, BR), F32), vm((16, 3, 1, BR), F32), vm((3, 1, BR), F32),
            vm((16,) + t4, BF), vm((3, 128, BR + SK), BF), vm((3, BR + SK, 128), BF),
            vm((ROWS * COLS, 128), F32), vm((ROWS * COLS, 128), F32), vm((32, BR), F32),
            dma((13,)), dma((3, 5)), dma((3, 3)), pltpu.SemaphoreType.REGULAR,
            dma((3, 4, 3)), dma((3, 4, 3)), dma((3, 2, 3)), dma((3, 2, 3)), dma((4, 3)), dma((4, 3)),
            dma((8,)), dma((8,)), dma((4,)), dma((4,)), dma((16,)), dma((16,)), dma((16,)), dma((16,)), dma((2,)), dma((2,)),
            vm((16, 4, 16, 128), F32), vm((16, 4, 16, 128), BF), vm((8, 4, 16, 128), BF),
            vm((8, 4, 16, 128), F32), vm((8, 4, 16, 128), BF), vm((8, 4, 16, 128), BF), dma((9,)), dma((9,)),
        ]
    )
    return pl.pallas_call(
        functools.partial(kernel, n_lon),
        out_shape=jax.ShapeDtypeStruct((ROWS, COLS, 16), BF),
        in_specs=[pl.BlockSpec(memory_space=pltpu.HBM)] * 13,
        out_specs=pl.BlockSpec(memory_space=pltpu.VMEM),
        scratch_shapes=scratch,
        compiler_params=pltpu.CompilerParams(
            collective_id=0, has_side_effects=True, vmem_limit_bytes=63 * 1024 * 1024
        ),
        name="aspp_head",
    )(features, w_point, w_dilated, w_pool, bn_scale, bn_shift, jnp.swapaxes(proj_weight, 1, 2), proj_scale, proj_shift, skip, jnp.swapaxes(merge_weight, 2, 3), merge_scale, merge_shift)


def solution(mesh):
    return jax.shard_map(
        body,
        mesh=mesh,
        in_specs=(
            P(None, "lon", "chan"),
            P("chan", None),
            P(None, None, None, "chan", None),
            P("chan", None),
            P(),
            P(),
            P(None, None, "chan"),
            P("chan"),
            P("chan"),
            P(None, "lon", None),
            P(None, None, None, "chan"),
            P("chan"),
            P("chan"),
        ),
        out_specs=P(None, "lon", "chan"),
        check_vma=False,
    )
```

```python
import functools

import jax
import jax.numpy as jnp
from jax import lax
from jax.experimental import pallas as pl
from jax.experimental.pallas import tpu as pltpu
from jax.sharding import PartitionSpec as P

BF = jnp.bfloat16
F32 = jnp.float32
MESH = pl.DeviceIdType.MESH

ROWS, COLS, CH, BR, SK = 48, 8, 128, 256, 48
OWN = 3
RIM = 36
DIL = (12, 24, 36)
CHUNKS = (
    ((((2, 0), 0, 3),), (((2, 2), 0, 3),), (((1, 0), 0, 3),)),
    ((((1, 2), 0, 3),), (((0, 0), 0, 3),), (((0, 2), 0, 3),)),
    (
        (((2, 1), 0, 3), ("point", 0, 1)),
        (((1, 1), 0, 3), ("point", 1, 2)),
        (((0, 1), 0, 3), ("point", 2, 3)),
    ),
)
TILES = [[sum(hi - lo for _, lo, hi in part) for part in chunk] for chunk in CHUNKS]
ORDERS = ((0, 2, 1), (2, 1, 0), (1, 0, 2))
LANES = ((0, 512), (512, 896), (896, 1280))
FAR = {(0, 0): (2, 1), (0, 2): (1, 2), (1, 0): (3, 4, 2), (1, 2): (3, 2, 4), (2, 0): (5, 4), (2, 2): (4, 5)}
FARTHEST = (7, 15, 5, 6, 13, 14, 3, 11, 4, 12, 1, 2, 9, 10, 8)
GRAY = ((0, 0), (0, 1), (1, 1), (1, 0))


def dot(a, b):
    return lax.dot_general(a, b, (((1,), (0,)), ((), ())), preferred_element_type=F32)


def dot_nt(a, b):
    return lax.dot_general(a, b, (((1,), (1,)), ((), ())), preferred_element_type=F32)


def to_tiles(v):
    n = v.shape[0] // 8
    lo = v[:, :128].reshape(n, 8, 128)
    hi = v[:, 128:].reshape(n, 8, 128)
    return jnp.concatenate([lo, hi], axis=1)


def from_tiles(t):
    n = t.shape[0]
    lo = t[:, :8].reshape(n * 8, 128)
    hi = t[:, 8:].reshape(n * 8, 128)
    return jnp.concatenate([lo, hi], axis=1)


class Several:
    def __init__(self):
        self.copies = []

    def wait(self):
        for cp in self.copies:
            cp.wait()


def kernel(
    n_lon,
    feat_h, wpt_h, wd_h, wpool_h, bns_h, bnt_h, pw_h, ps_h, pt_h, skip_h, mw_h, ms_h, mt_h,
    out_ref,
    *refs,
):
    (feat, wpt, wd, wpool, bns, bnt, ps, pt, skip, ms, mt, xs, xpad, hpad, edge, hedge), refs = refs[:16], refs[16:]
    steps, refs = refs[:108], refs[108:]
    (
        fin, sh, rsh, wt0, wt1, wt2, ia, ib, ic, img, gat, wrow, wcat, vskip, vskip_out, proj,
        ld_sem, pw_sem, mw_sem, known,
        rs_s, rs_r, sh_s, sh_r, wt_s, wt_r, ia_s, ia_r, ib_s, ib_r, ic_s, ic_r, ga_s, ga_r, ev_s, ev_r, hb, hbs, hc, hq, hqs, hr, hr_s, hr_r,
    ) = refs
    A0, SB0, R0 = ([[steps[(k * 3 + p) * 12 + i] for p in range(3)] for k in range(3)] for i in range(3))
    ACC, SB, RR = (
        [[[steps[(k * 3 + p) * 12 + 3 * (q + 1) + i] for p in range(3)] for k in range(3)] for q in range(3)] for i in range(3)
    )
    lon = lax.axis_index("lon")
    chan = lax.axis_index("chan")
    a = chan // 8
    y = (chan // 2) % 4
    c = chan % 2
    bit = (a, y // 2, (y % 2 + y // 2) % 2)
    beta = c * 8 + bit[0] * 4 + bit[1] * 2 + bit[2]

    loads = {}
    for i, (name, src, dst) in enumerate(
        [
            ("feat", feat_h, feat), ("wd2", wd_h.at[2], wd.at[2]), ("wd1", wd_h.at[1], wd.at[1]),
            ("wd0", wd_h.at[0], wd.at[0]), ("wpt", wpt_h, wpt), ("wpool", wpool_h, wpool),
            ("ps", ps_h, ps), ("pt", pt_h, pt), ("bns", bns_h, bns), ("bnt", bnt_h, bnt), ("skip", skip_h, skip),
            ("ms", ms_h, ms), ("mt", mt_h, mt),
        ]
    ):
        loads[name] = pltpu.make_async_copy(src, dst, ld_sem.at[i])
        if i < 3:
            loads[name].start()

    def chan_peer(m):
        mc, mx, mh, ml = (m >> 3) & 1, (m >> 2) & 1, (m >> 1) & 1, m & 1
        pc = 1 - c if mc else c
        pa = 1 - a if mx else a
        flip = y + 1 - 2 * (y % 2)
        py = {(0, 0): y, (0, 1): flip, (1, 0): 3 - y, (1, 1): (y + 2) % 4}[(mh, ml)]
        return (lon, pa * 8 + py * 2 + pc)

    def beta_peer(m):
        bits = [c, *bit]
        masks = [(m >> 3) & 1, (m >> 2) & 1, (m >> 1) & 1, m & 1]
        f = [1 - b if k else b for b, k in zip(bits, masks)]
        return f[0] * 8 + f[1] * 4 + f[2] * 2 + f[3]

    sibling = chan_peer(8)
    step_peer = (chan_peer(4), chan_peer(2), chan_peer(1))

    def lon_peer(k):
        return ((lon + k + n_lon) % n_lon, chan)

    def lon_xor(m):
        out = lon
        for p in range(5):
            if (m >> p) & 1:
                b = (lon // (1 << p)) % 2
                out = out + (1 - 2 * b) * (1 << p)
        return (out, chan)

    near = list(range(1, 8))
    blocks = n_lon // 8

    barrier = pltpu.get_barrier_semaphore()
    greeted = 0
    for dev in (
        ([lon_peer(8), lon_peer(-8)] if blocks > 1 else [])
        + [lon_peer(k) for k in (5, -5, 4, -4, 3, -3, 2, -2, 1, -1)]
        + [lon_xor(m) for m in near]
        + [chan_peer(m) for m in range(1, 16)]
    ):
        pl.semaphore_signal(barrier, inc=1, device_id=dev, device_id_type=MESH)
        greeted += 1

    for name in list(loads)[3:]:
        loads[name].start()
    for p, ((s, e), ref) in enumerate(zip(LANES, (wt0, wt1, wt2))):
        loads[f"wt{p}"] = Several()
        for b in range(5):
            lo, hi = max(b * BR, s), min(b * BR + BR, e)
            if lo < hi:
                cp = pltpu.make_async_copy(
                    pw_h.at[b, :, lo - b * BR : hi - b * BR],
                    ref.at[bit[0], bit[1], bit[2], c, :, lo - s : hi - s],
                    pw_sem.at[p, b],
                )
                cp.start()
                loads[f"wt{p}"].copies.append(cp)
    loads["mw"] = Several()
    for t in range(3):
        for b in range(3):
            cp = pltpu.make_async_copy(mw_h.at[t, b], wrow.at[t, 16 * b : 16 * b + 16], mw_sem.at[t, b])
            cp.start()
            loads["mw"].copies.append(cp)

    sends = []

    def send(src, dst, s, r, dev):
        cp = pltpu.make_async_remote_copy(
            src_ref=src, dst_ref=dst, send_sem=s, recv_sem=r, device_id=dev, device_id_type=MESH
        )
        cp.start()
        sends.append(cp)
        return cp

    def taps(ref, d):
        return jnp.concatenate([ref[(RIM + (t - 1) * d) * 8 : (RIM + (t - 1) * d + ROWS) * 8] for t in range(3)], axis=1)

    def field(which, ref):
        if which == "point":
            return to_tiles(dot(ref[RIM * 8 : (RIM + ROWS) * 8], wpt[...])).reshape(16, OWN, 16, 128)
        rate, tap = which
        res = dot(taps(ref, DIL[rate]), wd[rate, :, tap].reshape(3 * CH, BR))
        return to_tiles(res).reshape(16, OWN, 16, 128)

    hsent = []

    def outer_send():
        for f in range(4):
            rim = field("point" if f == 3 else (f, 1), hpad).reshape(16, OWN, 2, 8, 128)
            tile = rim[:, 0] + sum(
                pltpu.roll(rim[:, j].reshape(32, 8, 128), 2 * j, 1).reshape(16, 2, 8, 128) for j in range(1, OWN)
            )
            tile = tile.reshape(16, 16, 128)
            hb[:, f] = tile
            hbs[:, f] = tile.astype(BF)
        hsent.append(send(hbs.at[pl.ds((1 - c) * 8, 8)], hc, hr_s.at[8], hr_r.at[8], sibling))

    def outer_chips():
        hsent[0].wait_recv()
        hq[...] = hb[pl.ds(c * 8, 8)] + hc[...].astype(F32)
        hqs[...] = hq[...].astype(BF)
        for m in range(1, 8):
            hsent.append(send(hqs.at[beta_peer(m) - 8 * c], hr.at[m], hr_s.at[m], hr_r.at[m], chan_peer(m)))

    def outer_end():
        total = hq[beta - 8 * c]
        for m in range(1, 8):
            hsent[m].wait_recv()
            total = total + hr[m].astype(F32)
        for f in range(4):
            fin[f, OWN] = total[f]

    def compute(k):
        made = {}
        for p in range(3):
            at = 0
            for which, lo, hi in CHUNKS[k][p]:
                if which not in made:
                    made[which] = field(which, xpad)
                t = made[which][:, lo:hi].reshape(2, 2, 2, 2, hi - lo, 16, 128)
                A0[k][p][:, :, :, :, at : at + hi - lo] = t
                SB0[k][p][:, :, :, :, at : at + hi - lo] = t.astype(BF)
                at += hi - lo

    pending = {}

    def core_send(k):
        pending[k, 0] = [
            send(SB0[k][p].at[1 - c], R0[k][p], rs_s.at[k, 0, p], rs_r.at[k, 0, p], sibling) for p in range(3)
        ]

    def halve(k, step):
        sent = pending.pop((k, step))
        out = []
        for p in range(3):
            sent[p].wait_recv()
            left = [d for d in (0, 1, 2) if d not in ORDERS[p][:step]]
            mine = A0[k][p].at[c] if step == 0 else ACC[step - 1][k][p]
            got = R0[k][p] if step == 0 else RR[step - 1][k][p]
            d = ORDERS[p][step]

            def half(v):
                return tuple(v if q == d else slice(None) for q in left)

            there, here = half(1 - bit[d]), half(bit[d])
            SB[step][k][p][...] = (mine[there] + got[there].astype(F32)).astype(BF)
            out.append(
                send(SB[step][k][p], RR[step][k][p], rs_s.at[k, step + 1, p], rs_r.at[k, step + 1, p], step_peer[d])
            )
            ACC[step][k][p][...] = mine[here] + got[here].astype(F32)
        pending[k, step + 1] = out

    shifts = {}

    def finish(k):
        sent = pending.pop((k, 3))
        for p in range(3):
            sent[p].wait_recv()
            v = ACC[2][k][p][...] + RR[2][k][p][...].astype(F32)
            at = 0
            for which, lo, hi in CHUNKS[k][p]:
                part = v[at : at + hi - lo]
                at += hi - lo
                if which == "point":
                    fin[3, lo:hi] = part
                elif which[1] == 1:
                    fin[which[0], :OWN] = part
                else:
                    rate, tap = which
                    side, sign = (0, 1) if tap == 0 else (1, -1)
                    sh[rate, side] = part.astype(BF)
                    for j, dist in enumerate(FAR[which]):
                        shifts[rate, side, j] = send(
                            sh.at[rate, side], rsh.at[rate, side, j], sh_s.at[rate, side, j], sh_r.at[rate, side, j],
                            lon_peer(sign * dist),
                        )

    def weights(l0, l1):
        parts = []
        for (s, e), ref in zip(LANES, (wt0, wt1, wt2)):
            lo, hi = max(l0, s), min(l1, e)
            if lo < hi:
                parts.append(
                    jnp.concatenate(
                        [ref[q, GRAY[v][0], GRAY[v][1], w, :, lo - s : hi - s] for q in (0, 1) for v in range(4) for w in (0, 1)],
                        axis=0,
                    )
                )
        return parts[0] if len(parts) == 1 else jnp.concatenate(parts, axis=1)

    def project(branch, value):
        act = jnp.maximum(value * bns[branch : branch + 1] + bnt[branch : branch + 1], 0.0)
        return dot_nt(act.astype(BF), weights(branch * BR, branch * BR + BR))

    def branch_of(rate):
        sub = lax.broadcasted_iota(jnp.int32, (2, 8, 128), 1)
        col = lax.broadcasted_iota(jnp.int32, (2 * OWN, 8, 128), 1)
        total = fin[rate]
        for side, tap in ((0, 0), (1, 2)):
            tiles = []
            for j in range(len(FAR[rate, tap])):
                shifts[rate, side, j].wait_recv()
                tiles.append(rsh[rate, side, j].astype(F32).reshape(OWN, 2, 8, 128))
            if rate == 1:
                moved = tiles[0].reshape(OWN, 16, 128)
                west, east, w_col, e_col = tiles[1], tiles[2], 7, 0
            else:
                flat = [t.reshape(2 * OWN, 8, 128) for t in tiles]
                moved = pltpu.roll(jnp.where(col >= 4, flat[0], flat[1]), 4, 1).reshape(OWN, 16, 128)
                west, east, w_col, e_col = tiles[0], tiles[1], 3, 4
            rim = jnp.zeros((2, 8, 128), F32)
            for j in range(OWN):
                rim = jnp.where(sub == 2 * j, pltpu.roll(west[j], (2 * j - w_col) % 8, 1), rim)
                rim = jnp.where(sub == 2 * j + 1, pltpu.roll(east[j], (2 * j + 1 - e_col) % 8, 1), rim)
            total = total + jnp.concatenate([moved, rim.reshape(1, 16, 128)], axis=0)
        return project(1 + rate, from_tiles(total))

    WT = (wt0, wt1, wt2)
    wsent = {}

    def wt_step(step):
        for p in range(3):
            if step:
                wsent[step - 1, p].wait_recv()
            else:
                loads[f"wt{p}"].wait()
            done = ORDERS[p][:step]
            idx = tuple(slice(None) if d in done else bit[d] for d in range(3)) + (c,)
            ref = WT[p].at[idx]
            wsent[step, p] = send(ref, ref, wt_s.at[step, p], wt_r.at[step, p], step_peer[ORDERS[p][step]])

    def wt_core():
        for p in range(3):
            wsent[2, p].wait_recv()
            ref = WT[p].at[:, :, :, c]
            wsent[3, p] = send(ref, ref, wt_s.at[3, p], wt_r.at[3, p], sibling)

    isent = {}

    def image_start():
        loads["wpool"].wait()
        sums = jnp.sum(feat[...].astype(F32).reshape(ROWS * COLS, CH), axis=0, keepdims=True)
        hi = sums.astype(BF)
        rest = sums - hi.astype(F32)
        mid = rest.astype(BF)
        low = (rest - mid.astype(F32)).astype(BF)
        row = lax.broadcasted_iota(jnp.int32, (16, CH), 0)
        lhs = jnp.where(
            row == 0,
            hi.astype(F32),
            jnp.where(row == 1, mid.astype(F32), jnp.where(row == 2, low.astype(F32), 0.0)),
        ).astype(BF)
        loads["ps"].wait()
        loads["pt"].wait()
        lane = lax.broadcasted_iota(jnp.int32, (1, BR), 1) - chan * 16
        scale = jnp.zeros((1, BR), F32)
        shift = jnp.zeros((1, BR), F32)
        for i in range(16):
            scale = jnp.where(lane == i, ps[i], scale)
            shift = jnp.where(lane == i, pt[i], shift)
        ic[0, 0] = jnp.sum(dot(lhs, wpool[...]), axis=0, keepdims=True)
        ic[0, 1] = scale
        ic[0, 2] = shift

    def image_send():
        for m in range(1, 16):
            isent[2, m] = send(ic.at[0], ic.at[m], ic_s.at[m], ic_r.at[m], chan_peer(m))

    def image_near():
        for m in range(1, 16):
            isent[2, m].wait_recv()
        total = ic[0]
        for m in range(1, 16):
            total = total + ic[m]
        img[...] = total
        ia[0] = total[0]
        for m in near:
            isent[0, m] = send(ia.at[0], ia.at[m], ia_s.at[m], ia_r.at[m], lon_xor(m))

    def image_wide():
        for m in near:
            isent[0, m].wait_recv()
        total = ia[0]
        for m in near:
            total = total + ia[m]
        ib[0] = total
        if blocks > 1:
            pl.semaphore_wait(known, 1)
            for m in range(1, blocks):
                isent[1, m] = send(ib.at[0], ib.at[m], ib_s.at[m], ib_r.at[m], lon_peer(8 * m))

    def image_end():
        total = ib[0]
        for m in range(1, blocks):
            isent[1, m].wait_recv()
            total = total + ib[m]
        return total / (ROWS * COLS * n_lon)

    def tell_known():
        if blocks > 1:
            pl.semaphore_signal(known, inc=1, device_id=lon_peer(-8), device_id_type=MESH)

    esent = []

    def edge_send():
        loads["skip"].wait()
        xs[...] = jnp.zeros((ROWS * COLS, 2 * CH), BF)
        xs[:, :CH] = x2
        xs[:, CH : CH + SK] = skip[...].astype(F32).reshape(ROWS * COLS, SK).astype(BF)
        pick_r = lax.broadcasted_iota(jnp.int32, (ROWS, ROWS * COLS), 0)
        pick_c = lax.broadcasted_iota(jnp.int32, (ROWS, ROWS * COLS), 1)
        for i, col in enumerate((7, 0)):
            edge[i] = dot((pick_c == pick_r * 8 + col).astype(BF), xs[...]).astype(BF)

    def edge_start():
        for i, k in enumerate((1, -1)):
            esent.append(send(edge.at[i], hedge.at[i], ev_s.at[i], ev_r.at[i], lon_peer(k)))

    def edge_place():
        for e in esent:
            e.wait_recv()
        spread_r = lax.broadcasted_iota(jnp.int32, (ROWS * COLS, ROWS), 0)
        spread_c = lax.broadcasted_iota(jnp.int32, (ROWS * COLS, ROWS), 1)
        placed = sum(dot((spread_r == spread_c * 8 + i).astype(BF), hedge[i, :, :CH]) for i in range(2))
        hpad[RIM * 8 : (RIM + ROWS) * 8] = placed.astype(BF)

    def merge_prepare():
        loads["mw"].wait()
        wide_rows = (BR + SK, BR + SK)
        eye = (
            lax.broadcasted_iota(jnp.int32, wide_rows, 0) == lax.broadcasted_iota(jnp.int32, wide_rows, 1)
        ).astype(BF)
        for t in range(3):
            wrow[t, 48:] = jnp.zeros((80, BR + SK), BF)
            wcat[t] = dot_nt(eye, wrow[t]).astype(BF)
        vskip[...] = rows_shifted([dot(xs[:, CH : CH + SK], wcat[t, BR:]) for t in range(3)])
        spread_r = lax.broadcasted_iota(jnp.int32, (ROWS * COLS, ROWS), 0)
        spread_c = lax.broadcasted_iota(jnp.int32, (ROWS * COLS, ROWS), 1)
        outer = dot((spread_r == spread_c * 8 + 7).astype(BF), hedge[0, :, CH:]) + dot(
            (spread_r == spread_c * 8).astype(BF), hedge[1, :, CH:]
        )
        outer = outer[:, :SK].astype(BF)
        vskip_out[...] = rows_shifted([dot(outer, wcat[t, BR:]) for t in range(3)])

    def rows_shifted(parts):
        zero = jnp.zeros((8, 128), F32)
        n = ROWS * COLS
        up = jnp.concatenate([zero, parts[0][: n - 8]], axis=0)
        down = jnp.concatenate([parts[2][8:], zero], axis=0)
        return parts[1] + up + down

    loads["feat"].wait()
    x2 = feat[...].astype(F32).reshape(ROWS * COLS, CH).astype(BF)
    xpad[: RIM * 8] = jnp.zeros((RIM * 8, CH), BF)
    xpad[(RIM + ROWS) * 8 :] = jnp.zeros((RIM * 8, CH), BF)
    hpad[: RIM * 8] = jnp.zeros((RIM * 8, CH), BF)
    hpad[(RIM + ROWS) * 8 :] = jnp.zeros((RIM * 8, CH), BF)
    xpad[RIM * 8 : (RIM + ROWS) * 8] = x2
    image_start()
    edge_send()
    loads["wd2"].wait()
    loads["wd1"].wait()
    compute(0)
    pl.semaphore_wait(barrier, greeted)
    core_send(0)
    edge_start()
    loads["wd0"].wait()
    compute(1)
    core_send(1)
    image_send()
    halve(0, 0)
    loads["wpt"].wait()
    compute(2)
    core_send(2)
    halve(1, 0)
    halve(2, 0)
    wt_step(0)
    tell_known()
    halve(0, 1)
    halve(1, 1)
    halve(2, 1)
    wt_step(1)
    edge_place()
    outer_send()
    halve(0, 2)
    halve(1, 2)
    outer_chips()
    image_near()
    halve(2, 2)
    wt_step(2)
    finish(0)
    finish(1)
    finish(2)
    merge_prepare()
    wt_core()
    outer_end()
    image_wide()
    loads["bns"].wait()
    loads["bnt"].wait()
    loads["ms"].wait()
    loads["mt"].wait()
    for p in range(3):
        wsent[3, p].wait_recv()
    proj[...] = project(0, from_tiles(fin[3]))
    proj[...] += branch_of(0)
    proj[...] += branch_of(1)
    proj[...] += branch_of(2)
    gat[beta] = to_tiles(proj[...]).astype(BF)
    gsent = [send(gat.at[beta], gat.at[beta], ga_s.at[m], ga_r.at[m], chan_peer(m)) for m in FARTHEST]
    offset = project(4, jnp.broadcast_to(image_end(), (32, BR)))[:8]
    for g in gsent:
        g.wait_recv()

    def on_tiles(v):
        return to_tiles(jnp.broadcast_to(v, (8, BR)))[None]

    pooled = jnp.maximum((gat[...].astype(F32) + on_tiles(offset)) * on_tiles(img[1]) + on_tiles(img[2]), 0.0)
    pf = from_tiles(pooled[:, :OWN].reshape(ROWS, 16, 128)).astype(BF)
    rim = from_tiles(pooled[:, OWN]).astype(BF)
    v = vskip[...] + rows_shifted([dot(pf, wcat[t, :BR]) for t in range(3)])
    cell = lax.broadcasted_iota(jnp.int32, (ROWS * COLS, 128), 0)
    held = lax.broadcasted_iota(jnp.int32, (ROWS * COLS, 128), 1)
    row = cell // 8
    west_at = (row // OWN) * 8 + 2 * (row % OWN)
    take = ((cell % 8 == 7) & (held == west_at)) | ((cell % 8 == 0) & (held == west_at + 1))
    outer = dot(take.astype(BF), rim).astype(BF)
    vo = vskip_out[...] + rows_shifted([dot(outer, wcat[t, :BR]) for t in range(3)])
    v3 = v.reshape(ROWS, 8, 128)
    vo3 = vo.reshape(ROWS, 8, 128)
    col = lax.broadcasted_iota(jnp.int32, (ROWS, 8, 128), 1)
    mid = pltpu.roll(v3, 112, 2)
    left = pltpu.roll(jnp.where(col == 7, vo3, v3), 1, 1)
    right = pltpu.roll(pltpu.roll(jnp.where(col == 0, vo3, v3), 96, 2), 7, 1)
    total = mid + left + right
    lane = lax.broadcasted_iota(jnp.int32, (1, 1, 128), 2)
    scale = jnp.zeros((1, 1, 128), F32)
    shift = jnp.zeros((1, 1, 128), F32)
    for i in range(16):
        scale = jnp.where(lane == i, ms[i], scale)
        shift = jnp.where(lane == i, mt[i], shift)
    out_ref[...] = jnp.maximum(total * scale + shift, 0.0)[:, :, :16].astype(BF)
    for cp in sends:
        cp.wait_send()


def body(features, w_point, w_dilated, w_pool, bn_scale, bn_shift, proj_weight, proj_scale, proj_shift, skip, merge_weight, merge_scale, merge_shift):
    n_lon = lax.axis_size("lon")
    vm = pltpu.VMEM
    dma = pltpu.SemaphoreType.DMA
    t3, t4 = (OWN, 16, 128), (OWN + 1, 16, 128)
    steps = []
    for chunk in TILES:
        for n in chunk:
            for i, rest in enumerate(((2, 2, 2), (2, 2), (2,), ())):
                own = ((2,) + rest if i == 0 else rest) + (n, 16, 128)
                steps += [vm(own, F32), vm(own, BF), vm(rest + (n, 16, 128), BF)]
    scratch = (
        [
            vm((ROWS, COLS, CH), BF), vm((CH, BR), BF), vm((3, 3, 3, CH, BR), BF), vm((CH, BR), BF),
            vm((5, BR), F32), vm((5, BR), F32), pltpu.SMEM((16,), F32), pltpu.SMEM((16,), F32),
            vm((ROWS, COLS, SK), BF), pltpu.SMEM((16,), F32), pltpu.SMEM((16,), F32),
            vm((ROWS * COLS, 2 * CH), BF), vm(((ROWS + 2 * RIM) * 8, CH), BF), vm(((ROWS + 2 * RIM) * 8, CH), BF),
            vm((2, ROWS, 2 * CH), BF), vm((2, ROWS, 2 * CH), BF),
        ]
        + steps
        + [
            vm((4,) + t4, F32), vm((3, 2) + t3, BF), vm((3, 2, 3) + t3, BF),
            vm((2, 2, 2, 2, 16, 512), BF), vm((2, 2, 2, 2, 16, 384), BF), vm((2, 2, 2, 2, 16, 384), BF),
            vm((8, 1, BR), F32), vm((4, 1, BR), F32), vm((16, 3, 1, BR), F32), vm((3, 1, BR), F32),
            vm((16,) + t4, BF), vm((3, 128, BR + SK), BF), vm((3, BR + SK, 128), BF),
            vm((ROWS * COLS, 128), F32), vm((ROWS * COLS, 128), F32), vm((32, BR), F32),
            dma((13,)), dma((3, 5)), dma((3, 3)), pltpu.SemaphoreType.REGULAR,
            dma((3, 4, 3)), dma((3, 4, 3)), dma((3, 2, 3)), dma((3, 2, 3)), dma((4, 3)), dma((4, 3)),
            dma((8,)), dma((8,)), dma((4,)), dma((4,)), dma((16,)), dma((16,)), dma((16,)), dma((16,)), dma((2,)), dma((2,)),
            vm((16, 4, 16, 128), F32), vm((16, 4, 16, 128), BF), vm((8, 4, 16, 128), BF),
            vm((8, 4, 16, 128), F32), vm((8, 4, 16, 128), BF), vm((8, 4, 16, 128), BF), dma((9,)), dma((9,)),
        ]
    )
    return pl.pallas_call(
        functools.partial(kernel, n_lon),
        out_shape=jax.ShapeDtypeStruct((ROWS, COLS, 16), BF),
        in_specs=[pl.BlockSpec(memory_space=pltpu.HBM)] * 13,
        out_specs=pl.BlockSpec(memory_space=pltpu.VMEM),
        scratch_shapes=scratch,
        compiler_params=pltpu.CompilerParams(
            collective_id=0, has_side_effects=True, vmem_limit_bytes=63 * 1024 * 1024
        ),
        name="aspp_head",
    )(features, w_point, w_dilated, w_pool, bn_scale, bn_shift, jnp.swapaxes(proj_weight, 1, 2), proj_scale, proj_shift, skip, jnp.swapaxes(merge_weight, 2, 3), merge_scale, merge_shift)


def solution(mesh):
    return jax.shard_map(
        body,
        mesh=mesh,
        in_specs=(
            P(None, "lon", "chan"),
            P("chan", None),
            P(None, None, None, "chan", None),
            P("chan", None),
            P(),
            P(),
            P(None, None, "chan"),
            P("chan"),
            P("chan"),
            P(None, "lon", None),
            P(None, None, None, "chan"),
            P("chan"),
            P("chan"),
        ),
        out_specs=P(None, "lon", "chan"),
        check_vma=False,
    )
```
